32 devices in a mesh: tile: 8 (over y, x, core), agent: 4 (over z).
Axes of the slice: x: 2, y: 2, z: 4, core: 2. Of those that a mesh axis runs over, the one named last changes fastest.
Arguments:
- agent_state: float32 [4, 1, 16, 128, 256], P(None, None, None, 'tile', 'agent'), may hold values from 0 to 2
- measured: float32 [1, 16, 8192], P(None, None, ('tile', 'agent')), may hold values from 0 to 12
- bin_index: int32 [16, 128, 256], P(None, 'tile', 'agent'), may hold values from 64 to 446, as said below
- bin_frac: int32 [16, 128, 256], P(None, 'tile', 'agent'), may hold values from 0 to 723, as said below
- patch_offsets: int32 [3], replicated, may hold values from 1 to 15
- agent_weights: float32 [4], replicated, may hold values from 0.5 to 2
- up_weight: bfloat16 [3, 256, 4096], P(None, None, 'agent'), may hold values from -0.375 to 0.375
- down_weight: bfloat16 [3, 4096, 256], P(None, 'agent'), may hold values from -0.09375 to 0.09375
Outputs:
- state_next: float32 [4, 1, 16, 128, 256], P(None, None, None, 'tile', 'agent')
- data_fit: float32 [1, 16, 128, 256], P(None, None, 'tile', 'agent')
The draws below stay inside these ranges and needn't reach their ends.
Inputs may be any that keep to these rules, and one draw needn't show every extreme that they name: bin_index[a, x, y] = floor(((x - 64) c_a + (y - 128) s_a) / 724) + 256 and bin_frac[a, x, y] is the remainder of that division, for whole numbers c_a, s_a of size at most 724 with c_a * c_a + s_a * s_a close to 524176, one pair an angle. bin_frac is the remainder that belongs to bin_index.
All inputs are finite; a program needn't handle non-finite values.
Results may differ from the reference program's by a relative error of at most 0.0003.
The reference program's roundings to bfloat16 on the way count: a program that leaves them out, or rounds other values in their place, can miss the bound.
Values may be sent and summed in bfloat16 or wider, within the bound.
A program may use at most 64 MiB of HBM per device.

```python
import math
import jax
import jax.numpy as jnp
import numpy as np
from jax import lax

PATCH = 16
SLICES = 16
HIDDEN_SIZE = 4096
ANGLES = 16
GRAD_STEPS = 1
AGENTS = 4
TIMES = 1
NX = 128
NY = 256
BINS = 512
SINO = 8192


def geometry(key):
    turns = jax.random.randint(jax.random.fold_in(key, 11), (ANGLES,), 0, 4096)
    phases = np.arange(4096) * (2.0 * math.pi / 4096.0)
    cosines = jnp.asarray(np.floor(724.0 * np.cos(phases) + 0.5).astype(np.int32))
    sines = jnp.asarray(np.floor(724.0 * np.sin(phases) + 0.5).astype(np.int32))
    across = jnp.arange(NX, dtype=jnp.int32) - NX // 2
    along = jnp.arange(NY, dtype=jnp.int32) - NY // 2
    reach = cosines[turns][:, None, None] * across[None, :, None] + sines[turns][:, None, None] * along[None, None, :]
    return (reach // 724 + BINS // 2, reach % 724)


def draw_bin_index(key, part):
    return geometry(key)[0]


def draw_bin_frac(key, part):
    return geometry(key)[1]


def level_of(rng, shape, split, smallest, top_value):
    gain, own = 1.0, jax.random.fold_in(rng, 6)
    for dim, parts in split:
        steps = jnp.exp(jax.random.uniform(jax.random.fold_in(own, dim), (parts,), jnp.float32, smallest / len(split), top_value / len(split)))
        gain = gain * jnp.repeat(steps, shape[dim] // parts).reshape([-1 if axis == dim else 1 for axis in range(len(shape))])
    return gain


def normal_values(rng, shape, scale, most, split=(), kind=jnp.bfloat16):
    level = level_of(rng, shape, split, -0.22, 0.18) if split else 1.0
    entries = jax.random.normal(rng, shape, jnp.float32) * scale * level
    return jnp.minimum(jnp.maximum(entries, -most), most).astype(kind)


def setup_inputs(seed: int = 0) -> dict:
    key_of = jax.random.split(jax.random.key(seed), 9)
    agent_state = jnp.clip(2.0 * jax.random.uniform(key_of[0], (AGENTS, TIMES, SLICES, NX, NY), jnp.float32) ** level_of(key_of[0], (AGENTS, TIMES, SLICES, NX, NY), ((3, 8), (4, 4)), -0.2, 0.2), 0.0, 2.0)
    measured = jnp.clip(12.0 * jax.random.uniform(key_of[1], (TIMES, SLICES, SINO), jnp.float32) ** level_of(key_of[1], (TIMES, SLICES, SINO), ((2, 32),), -0.2, 0.2), 0.0, 12.0)
    bin_index = draw_bin_index(jax.random.fold_in(key_of[8], 71), 0)
    bin_frac = draw_bin_frac(jax.random.fold_in(key_of[8], 71), 0)
    patch_offsets = jax.random.randint(key_of[4], (AGENTS - 1,), 1, 16).astype(jnp.int32)
    agent_weights = jnp.clip(jnp.exp(jax.random.uniform(key_of[5], (AGENTS,), jnp.float32, math.log(0.5), math.log(2.0))), 0.5, 2.0)
    up_weight = normal_values(key_of[6], (AGENTS - 1, PATCH * PATCH, HIDDEN_SIZE), (PATCH * PATCH) ** -0.5, 0.375, ((2, 4),))
    down_weight = normal_values(key_of[7], (AGENTS - 1, HIDDEN_SIZE, PATCH * PATCH), HIDDEN_SIZE ** -0.5, 0.09375, ((1, 4),))
    return {"agent_state": agent_state, "measured": measured, "bin_index": bin_index, "bin_frac": bin_frac, "patch_offsets": patch_offsets, "agent_weights": agent_weights, "up_weight": up_weight, "down_weight": down_weight}


def network(patches, up_rows, down_rows):
    count = patches.shape[0]
    block = math.gcd(count, 4096)

    def apply_block(rows_in):
        hidden = jax.nn.relu(jnp.dot(rows_in, up_rows, preferred_element_type=jnp.float32)).astype(jnp.bfloat16)
        return jnp.dot(hidden, down_rows, preferred_element_type=jnp.float32)
    return lax.map(apply_block, patches.reshape(count // block, block, -1)).reshape(count, -1)

def data_agent(volume, measured, bin_index, bin_frac, factor):
    planes = volume.shape[0] * volume.shape[1]
    current = volume.reshape(planes, -1)
    lows = bin_index.reshape(ANGLES, -1)
    weights = bin_frac.reshape(ANGLES, -1).astype(jnp.float32) / 724.0
    target = measured.reshape(planes, ANGLES, BINS)
    for iteration in range(GRAD_STEPS):

        def project(carry, item):
            low_bin, weight = item
            row_sum = jnp.zeros((planes, BINS), jnp.float32)
            row_sum = row_sum.at[:, low_bin].add(current * weight[None, :])
            row_sum = row_sum.at[:, low_bin + 1].add(current * (1.0 - weight)[None, :])
            return (carry, row_sum)
        unused, sums = lax.scan(project, jnp.zeros((), jnp.float32), (lows, weights))
        misfit = factor * jnp.transpose(sums, (1, 0, 2)) - target

        def spread(total, item):
            low_bin, weight, resid = item
            total = total + jnp.take(resid, low_bin, axis=1) * weight[None, :]
            total = total + jnp.take(resid, low_bin + 1, axis=1) * (1.0 - weight)[None, :]
            return (total, None)
        back_sum, unused = lax.scan(spread, jnp.zeros_like(current), (lows, weights, jnp.transpose(misfit, (1, 0, 2))))
        current = current - factor * back_sum
    return current.reshape(volume.shape)

def in_plane(volume, shift, up_rows, down_rows):
    n_time, n_slice, n_row, n_col = volume.shape
    rolled = jnp.roll(volume, (-shift, -shift), axis=(2, 3))
    patches = rolled.reshape(n_time, n_slice, n_row // PATCH, PATCH, n_col // PATCH, PATCH)
    patches = patches.transpose(0, 1, 2, 4, 3, 5).reshape(-1, PATCH * PATCH)
    result = network(patches, up_rows, down_rows)
    result = result.reshape(n_time, n_slice, n_row // PATCH, n_col // PATCH, PATCH, PATCH)
    result = result.transpose(0, 1, 2, 4, 3, 5).reshape(n_time, n_slice, n_row, n_col)
    return jnp.roll(result, (shift, shift), axis=(2, 3))

def along_rows(volume, shift, up_rows, down_rows):
    n_time, n_slice, n_row, n_col = volume.shape
    rolled = jnp.roll(volume, -shift, axis=2)
    patches = rolled.reshape(n_time, n_slice, n_row // PATCH, PATCH, n_col)
    patches = patches.transpose(0, 2, 4, 1, 3).reshape(-1, n_slice * PATCH)
    result = network(patches, up_rows, down_rows)
    result = result.reshape(n_time, n_row // PATCH, n_col, n_slice, PATCH)
    result = result.transpose(0, 3, 1, 4, 2).reshape(n_time, n_slice, n_row, n_col)
    return jnp.roll(result, shift, axis=2)

def along_cols(volume, shift, up_rows, down_rows):
    n_time, n_slice, n_row, n_col = volume.shape
    rolled = jnp.roll(volume, -shift, axis=3)
    patches = rolled.reshape(n_time, n_slice, n_row, n_col // PATCH, PATCH)
    patches = patches.transpose(0, 2, 3, 1, 4).reshape(-1, n_slice * PATCH)
    result = network(patches, up_rows, down_rows)
    result = result.reshape(n_time, n_row, n_col // PATCH, n_slice, PATCH)
    result = result.transpose(0, 3, 1, 2, 4).reshape(n_time, n_slice, n_row, n_col)
    return jnp.roll(result, shift, axis=3)

def reference(agent_state, measured, bin_index, bin_frac, patch_offsets, agent_weights, up_weight, down_weight):
    factor = 1.0 / math.sqrt(ANGLES * (NX + NY))
    data_fit = data_agent(agent_state[0], measured, bin_index, bin_frac, factor)
    noisy = agent_state[1:].astype(jnp.bfloat16)
    first = agent_state[1] - in_plane(noisy[0], patch_offsets[0], up_weight[0], down_weight[0])
    second = agent_state[2] - along_rows(noisy[1], patch_offsets[1], up_weight[1], down_weight[1])
    third = agent_state[3] - along_cols(noisy[2], patch_offsets[2], up_weight[2], down_weight[2])
    answers = jnp.stack([data_fit, first, second, third])
    joining = agent_weights / jnp.sum(agent_weights)
    joined = lax.optimization_barrier(jnp.sum(joining[:, None, None, None, None] * (2.0 * answers - agent_state), axis=0))
    state_next = agent_state + joined[None] - answers
    return (state_next, data_fit)
```

```python
import functools
import math

import jax
import jax.numpy as jnp
from jax import lax
from jax.experimental import pallas as pl
from jax.experimental.pallas import tpu as pltpu
from jax.sharding import PartitionSpec as P

PATCH = 16
LANES = 128
DENOM = 724.0


def split_pair(values):
    high = values.astype(jnp.bfloat16)
    low = (values - high.astype(jnp.float32)).astype(jnp.bfloat16)
    return high, low


def interpolation_rows(low_ref, frac_ref, angle, start, window):
    lows = low_ref[pl.ds(angle, 1), :] - start
    near = frac_ref[pl.ds(angle, 1), :].astype(jnp.float32) / DENOM
    far = 1.0 - near
    near_high = near.astype(jnp.bfloat16).astype(jnp.float32)
    far_high = far.astype(jnp.bfloat16).astype(jnp.float32)
    near_low, far_low = near - near_high, far - far_high
    apart = lax.broadcasted_iota(jnp.int32, (window, lows.shape[1]), 0) - lows
    at_near, at_far = apart == 0, apart == 1
    high = jnp.where(at_near, near_high, jnp.where(at_far, far_high, 0.0))
    low = jnp.where(at_near, near_low, jnp.where(at_far, far_low, 0.0))
    return jnp.concatenate([high.astype(jnp.bfloat16), low.astype(jnp.bfloat16)], axis=0)


def project_kernel(factor, window, starts_ref, volume_ref, low_ref, frac_ref, sino_ref):
    angles, planes, bins = sino_ref.shape
    high, low = split_pair(volume_ref[...])
    stacked = jnp.concatenate([high, low], axis=0)

    def step(angle, carry):
        start = starts_ref[angle]
        rows = interpolation_rows(low_ref, frac_ref, angle, start, window)
        out = lax.dot_general(
            stacked, rows, (((1,), (1,)), ((), ())), preferred_element_type=jnp.float32
        )
        out = out[:planes] + out[planes:]
        out = factor * (out[:, :window] + out[:, window:])
        if bins > window:
            out = jnp.concatenate([out, jnp.zeros((planes, bins - window), jnp.float32)], axis=1)
            out = pltpu.roll(out, start, 1)
        sino_ref[angle] = out
        return carry

    lax.fori_loop(0, angles, step, 0)


def spread_kernel(factor, window, starts_ref, misfit_ref, low_ref, frac_ref, volume_ref, out_ref):
    angles, planes, bins = misfit_ref.shape
    out_ref[...] = volume_ref[...]

    def step(angle, carry):
        start = starts_ref[angle]
        rows = interpolation_rows(low_ref, frac_ref, angle, start, window)
        resid = misfit_ref[angle]
        if bins > window:
            resid = pltpu.roll(resid, bins - start, 1)[:, :window]
        high, low = split_pair(resid)
        left = jnp.concatenate([high, low], axis=0)
        left = jnp.concatenate([left, left], axis=1)
        out = jnp.dot(left, rows, preferred_element_type=jnp.float32)
        out_ref[...] -= factor * (out[:planes] + out[planes:])
        return carry

    lax.fori_loop(0, angles, step, 0)


def data_agent(volume, bin_index, bin_frac, measured, factor, sino_width):
    angles = bin_index.shape[0]
    planes = volume.shape[0] * volume.shape[1]
    current = volume.reshape(planes, -1)
    bins = sino_width // angles
    window = -(-(bin_index.shape[1] + bin_index.shape[2] + 2) // LANES) * LANES
    window = min(window, bins)
    lows = bin_index.reshape(angles, -1)
    fracs = bin_frac.reshape(angles, -1)
    corners = bin_index[:, :: bin_index.shape[1] - 1, :: bin_index.shape[2] - 1]
    starts = jnp.minimum(jnp.min(corners, axis=(1, 2)), bins - window)
    whole = pl.BlockSpec(memory_space=pltpu.VMEM)
    scalars = pl.BlockSpec(memory_space=pltpu.SMEM)
    cost = pl.CostEstimate(
        flops=4 * angles * window * current.shape[1] * planes * 2,
        bytes_accessed=3 * current.size * 4,
        transcendentals=0,
    )
    grant = pltpu.CompilerParams(vmem_limit_bytes=48 * 2**20)
    sino = pl.pallas_call(
        functools.partial(project_kernel, factor, window),
        out_shape=jax.ShapeDtypeStruct((angles, planes, bins), jnp.float32),
        in_specs=[scalars, whole, whole, whole],
        out_specs=whole,
        cost_estimate=cost,
        compiler_params=grant,
        name="project",
    )(starts, current, lows, fracs)
    partial_sino = jnp.transpose(sino, (1, 0, 2)).reshape(planes, -1)
    by_tile = lax.psum_scatter(partial_sino, "tile", scatter_dimension=1, tiled=True)
    owned_bins = lax.psum_scatter(by_tile, "agent", scatter_dimension=1, tiled=True)
    misfit = owned_bins - measured.reshape(planes, -1)
    band_bins = lax.all_gather(misfit, "agent", axis=1, tiled=True)
    all_bins = lax.all_gather(band_bins, "tile", axis=1, tiled=True)
    by_angle = jnp.transpose(all_bins.reshape(planes, angles, bins), (1, 0, 2))
    result = pl.pallas_call(
        functools.partial(spread_kernel, factor, window),
        out_shape=jax.ShapeDtypeStruct(current.shape, jnp.float32),
        in_specs=[scalars, whole, whole, whole, whole],
        out_specs=whole,
        cost_estimate=cost,
        compiler_params=grant,
        name="spread",
    )(starts, by_angle, lows, fracs, current)
    return result.reshape(volume.shape)


def roll_by(block, shift, axis):
    head = lax.slice_in_dim(block, 0, PATCH, axis=axis)
    return lax.dynamic_slice_in_dim(
        jnp.concatenate([block, head], axis=axis), shift, block.shape[axis], axis
    )


def roll_back(block, shift, axis):
    tail = lax.slice_in_dim(block, block.shape[axis] - PATCH, None, axis=axis)
    return lax.dynamic_slice_in_dim(
        jnp.concatenate([tail, block], axis=axis), PATCH - shift, block.shape[axis], axis
    )


def denoisers(noisy, offsets, up_weight, down_weight):
    tiles = lax.axis_size("tile")
    ahead = [(i, (i + 1) % tiles) for i in range(tiles)]
    behind = [((i + 1) % tiles, i) for i in range(tiles)]
    count, slices, rows, cols = noisy.shape
    below = lax.ppermute(noisy[:2, :, :PATCH], "tile", behind)
    both = jnp.concatenate([noisy[:2], below], axis=2)
    first = lax.dynamic_slice_in_dim(both[0], offsets[0], rows, 1)
    second = lax.dynamic_slice_in_dim(both[1], offsets[1], rows, 1)
    wide = lax.all_gather(jnp.stack([first, second, noisy[2]]), "agent", axis=3, tiled=True)
    width = wide.shape[3]
    row_blocks, col_blocks = rows // PATCH, width // PATCH

    def net(which, patches):
        hidden = jax.nn.relu(
            jnp.dot(patches, up_weight[which], preferred_element_type=jnp.float32)
        ).astype(jnp.bfloat16)
        return jnp.dot(hidden, down_weight[which], preferred_element_type=jnp.float32)

    patches = roll_by(wide[0], offsets[0], 2)
    patches = patches.reshape(slices, row_blocks, PATCH, col_blocks, PATCH)
    patches = patches.transpose(0, 1, 3, 2, 4).reshape(-1, PATCH * PATCH)
    terms = net(0, patches).reshape(slices, row_blocks, col_blocks, PATCH, PATCH)
    terms = terms.transpose(0, 1, 3, 2, 4).reshape(slices, rows, width)
    out_0 = roll_back(terms, offsets[0], 2)

    patches = wide[1].reshape(slices, row_blocks, PATCH, width)
    patches = patches.transpose(1, 3, 0, 2).reshape(-1, slices * PATCH)
    terms = net(1, patches).reshape(row_blocks, width, slices, PATCH)
    out_1 = terms.transpose(2, 0, 3, 1).reshape(slices, rows, width)

    patches = roll_by(wide[2], offsets[2], 2)
    patches = patches.reshape(slices, rows, col_blocks, PATCH)
    patches = patches.transpose(1, 2, 0, 3).reshape(-1, slices * PATCH)
    terms = net(2, patches).reshape(rows, col_blocks, slices, PATCH)
    terms = terms.transpose(2, 0, 1, 3).reshape(slices, rows, width)
    out_2 = roll_back(terms, offsets[2], 2)

    outs = lax.psum_scatter(
        jnp.stack([out_0, out_1, out_2]), "agent", scatter_dimension=3, tiled=True
    )
    above = lax.ppermute(outs[:2, :, rows - PATCH :], "tile", ahead)
    both = jnp.concatenate([above, outs[:2]], axis=2)
    first = lax.dynamic_slice_in_dim(both[0], PATCH - offsets[0], rows, 1)
    second = lax.dynamic_slice_in_dim(both[1], PATCH - offsets[1], rows, 1)
    return jnp.stack([first, second, outs[2]])


def shards(
    agent_state, measured, bin_index, bin_frac, patch_offsets, agent_weights, up_weight, down_weight
):
    row_count = agent_state.shape[3]
    col_count = agent_state.shape[4]
    tile_count = lax.axis_size("tile")
    agent_count = lax.axis_size("agent")
    full_rows = row_count * tile_count
    full_cols = col_count * agent_count
    angles = bin_index.shape[0]
    factor = 1.0 / math.sqrt(angles * (full_rows + full_cols))
    sino_width = measured.shape[2] * tile_count * agent_count
    data_fit = data_agent(agent_state[0], bin_index, bin_frac, measured, factor, sino_width)
    times, slices = agent_state.shape[1], agent_state.shape[2]
    noisy = agent_state[1:].astype(jnp.bfloat16)
    removed = jnp.stack(
        [denoisers(noisy[:, t], patch_offsets, up_weight, down_weight) for t in range(times)], axis=1
    )
    answers = jnp.concatenate([data_fit[None], agent_state[1:] - removed])
    joining = agent_weights / jnp.sum(agent_weights)
    joined = jnp.sum(joining[:, None, None, None, None] * (2.0 * answers - agent_state), axis=0)
    state_next = agent_state + joined[None] - answers
    return (state_next, data_fit)


def solution(mesh):
    placed = (
        P(None, None, None, "tile", "agent"),
        P(None, None, ("tile", "agent")),
        P(None, "tile", "agent"),
        P(None, "tile", "agent"),
        P(),
        P(),
        P(None, None, "agent"),
        P(None, "agent", None),
    )
    return jax.shard_map(
        shards,
        mesh=mesh,
        in_specs=placed,
        out_specs=(P(None, None, None, "tile", "agent"), P(None, None, "tile", "agent")),
        check_vma=False,
    )
```

```python
import functools
import math

import jax
import jax.numpy as jnp
from jax import lax
from jax.experimental import pallas as pl
from jax.experimental.pallas import tpu as pltpu
from jax.sharding import PartitionSpec as P

PATCH = 16
LANES = 128
DENOM = 724.0


def split_pair(values):
    high = values.astype(jnp.bfloat16)
    low = (values - high.astype(jnp.float32)).astype(jnp.bfloat16)
    return high, low


def interpolation_rows(low_ref, frac_ref, angle, start, window):
    lows = low_ref[pl.ds(angle, 1), :] - start
    near = frac_ref[pl.ds(angle, 1), :].astype(jnp.float32) / DENOM
    far = 1.0 - near
    near_high = near.astype(jnp.bfloat16).astype(jnp.float32)
    far_high = far.astype(jnp.bfloat16).astype(jnp.float32)
    near_low, far_low = near - near_high, far - far_high
    apart = lax.broadcasted_iota(jnp.int32, (window, lows.shape[1]), 0) - lows
    at_near, at_far = apart == 0, apart == 1
    high = jnp.where(at_near, near_high, jnp.where(at_far, far_high, 0.0))
    low = jnp.where(at_near, near_low, jnp.where(at_far, far_low, 0.0))
    return jnp.concatenate([high.astype(jnp.bfloat16), low.astype(jnp.bfloat16)], axis=0)


def project_kernel(factor, window, starts_ref, volume_ref, low_ref, frac_ref, sino_ref):
    angles, planes, bins = sino_ref.shape
    high, low = split_pair(volume_ref[...])
    stacked = jnp.concatenate([high, low], axis=0)

    def step(angle, carry):
        start = starts_ref[angle]
        rows = interpolation_rows(low_ref, frac_ref, angle, start, window)
        out = lax.dot_general(
            stacked, rows, (((1,), (1,)), ((), ())), preferred_element_type=jnp.float32
        )
        out = out[:planes] + out[planes:]
        out = factor * (out[:, :window] + out[:, window:])
        if bins > window:
            out = jnp.concatenate([out, jnp.zeros((planes, bins - window), jnp.float32)], axis=1)
            out = pltpu.roll(out, start, 1)
        sino_ref[angle] = out
        return carry

    lax.fori_loop(0, angles, step, 0)


def spread_kernel(factor, window, starts_ref, misfit_ref, low_ref, frac_ref, volume_ref, out_ref):
    angles, planes, bins = misfit_ref.shape
    out_ref[...] = volume_ref[...]

    def step(angle, carry):
        start = starts_ref[angle]
        rows = interpolation_rows(low_ref, frac_ref, angle, start, window)
        resid = misfit_ref[angle]
        if bins > window:
            resid = pltpu.roll(resid, bins - start, 1)[:, :window]
        high, low = split_pair(resid)
        left = jnp.concatenate([high, low], axis=0)
        left = jnp.concatenate([left, left], axis=1)
        out = jnp.dot(left, rows, preferred_element_type=jnp.float32)
        out_ref[...] -= factor * (out[:planes] + out[planes:])
        return carry

    lax.fori_loop(0, angles, step, 0)


def exchange_kernel(
    chunks_ref, target_ref, patches_ref, up_ref, down_ref, misfit_ref, nets_ref,
    tile_parts, band, agent_parts, every, wide, terms, term_parts,
    tile_send, tile_recv, sum_send, sum_recv, own_send, own_recv,
    every_send, every_recv, patch_send, patch_recv, term_send, term_recv,
):
    tiles, agents = chunks_ref.shape[0], chunks_ref.shape[1]
    tile, agent = lax.axis_index("tile"), lax.axis_index("agent")

    def tile_at(step):
        return lax.rem(tile + step, tiles)

    def agent_at(step):
        return lax.rem(agent + step, agents)

    def copy(source, target, send, recv, step, to):
        return pltpu.make_async_remote_copy(
            src_ref=source,
            dst_ref=target,
            send_sem=send.at[step],
            recv_sem=recv.at[step],
            device_id=to,
            device_id_type=pl.DeviceIdType.MESH,
        )

    def to_tile(step):
        return (tile_at(step), agent)

    def to_agent(step):
        return (tile, agent_at(step))

    def over(count, body):
        def step_body(step, carry):
            body(step)
            return carry

        lax.fori_loop(1, count, step_body, 0)

    barrier = pltpu.get_barrier_semaphore()
    over(agents, lambda step: pl.semaphore_signal(
        barrier, inc=1, device_id=to_agent(step), device_id_type=pl.DeviceIdType.MESH))
    over(tiles, lambda step: pl.semaphore_signal(
        barrier, inc=1, device_id=to_tile(step), device_id_type=pl.DeviceIdType.MESH))
    pl.semaphore_wait(barrier, tiles + agents - 2)

    def tile_copy(step):
        return copy(
            chunks_ref.at[tile_at(step)], tile_parts.at[step], tile_send, tile_recv, step,
            to_tile(step))

    def patch_copy(step):
        return copy(patches_ref, wide.at[step], patch_send, patch_recv, step, to_agent(step))

    def sum_copy(step):
        return copy(
            band.at[agent_at(step)], agent_parts.at[step], sum_send, sum_recv, step,
            to_agent(step))

    def own_copy(step):
        return copy(
            every.at[tile, agent], every.at[tile, agent], own_send, own_recv, step,
            to_agent(step))

    def own_arrival(step):
        where = every.at[tile, agent_at(agents - step)]
        return copy(where, where, own_send, own_recv, step, to_agent(step))

    def every_copy(step):
        return copy(
            every.at[tile], every.at[tile], every_send, every_recv, step, to_tile(step))

    def every_arrival(step):
        where = every.at[tile_at(tiles - step)]
        return copy(where, where, every_send, every_recv, step, to_tile(step))

    def term_copy(step):
        return copy(
            terms.at[agents - step], term_parts.at[step], term_send, term_recv, step,
            to_agent(step))

    over(tiles, lambda step: tile_copy(step).start())
    over(agents, lambda step: patch_copy(step).start())
    wide[0] = patches_ref[...]
    band[...] = chunks_ref[tile]

    def add_tile(step):
        tile_copy(step).wait_recv()
        band[...] += tile_parts[step]

    over(tiles, add_tile)
    over(agents, lambda step: sum_copy(step).start())
    every[tile, agent] = band[agent] - target_ref[...]

    def add_agent(step):
        sum_copy(step).wait_recv()
        every[tile, agent] += agent_parts[step]

    over(agents, add_agent)
    over(agents, lambda step: own_copy(step).start())

    over(agents, lambda step: patch_copy(step).wait_recv())
    count = patches_ref.shape[1]
    for which in range(patches_ref.shape[0]):
        rows = wide[:, which].reshape(agents * count, patches_ref.shape[2])
        hidden = jnp.dot(rows, up_ref[which], preferred_element_type=jnp.float32)
        hidden = jnp.maximum(hidden, 0.0).astype(jnp.bfloat16)
        out = jnp.dot(hidden, down_ref[which], preferred_element_type=jnp.float32)
        terms[:, which] = out.reshape(agents, count, out.shape[1])
    over(agents, lambda step: term_copy(step).start())

    over(agents, lambda step: own_arrival(step).wait_recv())
    over(tiles, lambda step: every_copy(step).start())
    over(tiles, lambda step: every_arrival(step).wait_recv())
    misfit_ref[...] = every[...]
    nets_ref[...] = terms[0]

    def add_terms(step):
        term_copy(step).wait_recv()
        nets_ref[...] += term_parts[step]

    over(agents, add_terms)
    over(tiles, lambda step: tile_copy(step).wait_send())
    over(agents, lambda step: patch_copy(step).wait_send())
    over(agents, lambda step: sum_copy(step).wait_send())
    over(agents, lambda step: own_copy(step).wait_send())
    over(tiles, lambda step: every_copy(step).wait_send())
    over(agents, lambda step: term_copy(step).wait_send())


def exchange(chunks, target, patches, up_weight, down_weight):
    tiles, agents, planes, own = chunks.shape
    whole = pl.BlockSpec(memory_space=pltpu.VMEM)
    nets = jax.ShapeDtypeStruct(patches.shape, jnp.float32)
    sems = [pltpu.SemaphoreType.DMA((n,)) for n in (
        tiles, tiles, agents, agents, agents, agents, tiles, tiles, agents, agents, agents, agents)]
    return pl.pallas_call(
        exchange_kernel,
        out_shape=(jax.ShapeDtypeStruct(chunks.shape, jnp.float32), nets),
        in_specs=[whole] * 5,
        out_specs=(whole, whole),
        scratch_shapes=[
            pltpu.VMEM(chunks.shape, jnp.float32),
            pltpu.VMEM((agents, planes, own), jnp.float32),
            pltpu.VMEM((agents, planes, own), jnp.float32),
            pltpu.VMEM(chunks.shape, jnp.float32),
            pltpu.VMEM((agents,) + patches.shape, jnp.bfloat16),
            pltpu.VMEM((agents,) + patches.shape, jnp.float32),
            pltpu.VMEM((agents,) + patches.shape, jnp.float32),
            *sems,
        ],
        compiler_params=pltpu.CompilerParams(
            collective_id=0, has_side_effects=True, vmem_limit_bytes=48 * 2**20
        ),
        name="exchange",
    )(chunks, target, patches, up_weight, down_weight)


def from_next(block, axis):
    count = lax.axis_size(axis)
    return lax.ppermute(block, axis, [((i + 1) % count, i) for i in range(count)])


def from_previous(block, axis):
    count = lax.axis_size(axis)
    return lax.ppermute(block, axis, [(i, (i + 1) % count) for i in range(count)])


def make_patches(noisy, offsets):
    rows, cols = noisy.shape[3], noisy.shape[4]
    times, slices = noisy.shape[1], noisy.shape[2]
    row_blocks, col_blocks = rows // PATCH, cols // PATCH
    below = from_next(noisy[:2, :, :, :PATCH], "tile")
    both = jnp.concatenate([noisy[:2], below], axis=3)
    first = lax.dynamic_slice_in_dim(both[0], offsets[0], rows, 2)
    second = lax.dynamic_slice_in_dim(both[1], offsets[1], rows, 2)
    sides = jnp.stack([first, noisy[2]])
    beyond = from_next(sides[..., :PATCH], "agent")
    both = jnp.concatenate([sides, beyond], axis=4)
    first = lax.dynamic_slice_in_dim(both[0], offsets[0], cols, 3)
    third = lax.dynamic_slice_in_dim(both[1], offsets[2], cols, 3)
    first = first.reshape(times, slices, row_blocks, PATCH, col_blocks, PATCH)
    first = first.transpose(0, 1, 2, 4, 3, 5).reshape(-1, PATCH * PATCH)
    second = second.reshape(times, slices, row_blocks, PATCH, cols)
    second = second.transpose(0, 2, 4, 1, 3).reshape(-1, slices * PATCH)
    third = third.reshape(times, slices, rows, col_blocks, PATCH)
    third = third.transpose(0, 2, 3, 1, 4).reshape(-1, slices * PATCH)
    return jnp.stack([first, second, third])


def place_patches(nets, offsets, shape):
    times, slices, rows, cols = shape
    row_blocks, col_blocks = rows // PATCH, cols // PATCH
    first = nets[0].reshape(times, slices, row_blocks, col_blocks, PATCH, PATCH)
    first = first.transpose(0, 1, 2, 4, 3, 5).reshape(shape)
    second = nets[1].reshape(times, row_blocks, cols, slices, PATCH)
    second = second.transpose(0, 3, 1, 4, 2).reshape(shape)
    third = nets[2].reshape(times, rows, col_blocks, slices, PATCH)
    third = third.transpose(0, 3, 1, 2, 4).reshape(shape)
    sides = jnp.stack([first, third])
    before = from_previous(sides[..., cols - PATCH :], "agent")
    both = jnp.concatenate([before, sides], axis=4)
    first = lax.dynamic_slice_in_dim(both[0], PATCH - offsets[0], cols, 3)
    third = lax.dynamic_slice_in_dim(both[1], PATCH - offsets[2], cols, 3)
    sides = jnp.stack([first, second])
    above = from_previous(sides[:, :, :, rows - PATCH :], "tile")
    both = jnp.concatenate([above, sides], axis=3)
    first = lax.dynamic_slice_in_dim(both[0], PATCH - offsets[0], rows, 2)
    second = lax.dynamic_slice_in_dim(both[1], PATCH - offsets[1], rows, 2)
    return jnp.stack([first, second, third])


def data_and_nets(
    volume, bin_index, bin_frac, measured, factor, patches, up_weight, down_weight
):
    angles = bin_index.shape[0]
    planes = volume.shape[0] * volume.shape[1]
    current = volume.reshape(planes, -1)
    tiles, agents, own = lax.axis_size("tile"), lax.axis_size("agent"), measured.shape[2]
    bins = tiles * agents * own // angles
    window = -(-(bin_index.shape[1] + bin_index.shape[2] + 2) // LANES) * LANES
    window = min(window, bins)
    lows = bin_index.reshape(angles, -1)
    fracs = bin_frac.reshape(angles, -1)
    corners = bin_index[:, :: bin_index.shape[1] - 1, :: bin_index.shape[2] - 1]
    starts = jnp.minimum(jnp.min(corners, axis=(1, 2)), bins - window)
    whole = pl.BlockSpec(memory_space=pltpu.VMEM)
    scalars = pl.BlockSpec(memory_space=pltpu.SMEM)
    cost = pl.CostEstimate(
        flops=4 * angles * window * current.shape[1] * planes * 2,
        bytes_accessed=3 * current.size * 4,
        transcendentals=0,
    )
    grant = pltpu.CompilerParams(vmem_limit_bytes=48 * 2**20)
    sino = pl.pallas_call(
        functools.partial(project_kernel, factor, window),
        out_shape=jax.ShapeDtypeStruct((angles, planes, bins), jnp.float32),
        in_specs=[scalars, whole, whole, whole],
        out_specs=whole,
        cost_estimate=cost,
        compiler_params=grant,
        name="project",
    )(starts, current, lows, fracs)
    chunks = jnp.transpose(sino, (1, 0, 2)).reshape(planes, tiles, agents, own)
    chunks = jnp.transpose(chunks, (1, 2, 0, 3))
    misfit, nets = exchange(
        chunks, measured.reshape(planes, own), patches, up_weight, down_weight
    )
    by_angle = jnp.transpose(misfit, (2, 0, 1, 3)).reshape(planes, angles, bins)
    by_angle = jnp.transpose(by_angle, (1, 0, 2))
    result = pl.pallas_call(
        functools.partial(spread_kernel, factor, window),
        out_shape=jax.ShapeDtypeStruct(current.shape, jnp.float32),
        in_specs=[scalars, whole, whole, whole, whole],
        out_specs=whole,
        cost_estimate=cost,
        compiler_params=grant,
        name="spread",
    )(starts, by_angle, lows, fracs, current)
    return result.reshape(volume.shape), nets


def shards(
    agent_state, measured, bin_index, bin_frac, patch_offsets, agent_weights, up_weight, down_weight
):
    row_count = agent_state.shape[3]
    col_count = agent_state.shape[4]
    tile_count = lax.axis_size("tile")
    agent_count = lax.axis_size("agent")
    full_rows = row_count * tile_count
    full_cols = col_count * agent_count
    angles = bin_index.shape[0]
    factor = 1.0 / math.sqrt(angles * (full_rows + full_cols))
    patches = make_patches(agent_state[1:].astype(jnp.bfloat16), patch_offsets)
    data_fit, nets = data_and_nets(
        agent_state[0], bin_index, bin_frac, measured, factor, patches, up_weight, down_weight
    )
    removed = place_patches(nets, patch_offsets, agent_state.shape[1:])
    answers = jnp.concatenate([data_fit[None], agent_state[1:] - removed])
    joining = agent_weights / jnp.sum(agent_weights)
    joined = jnp.sum(joining[:, None, None, None, None] * (2.0 * answers - agent_state), axis=0)
    state_next = agent_state + joined[None] - answers
    return (state_next, data_fit)


def solution(mesh):
    placed = (
        P(None, None, None, "tile", "agent"),
        P(None, None, ("tile", "agent")),
        P(None, "tile", "agent"),
        P(None, "tile", "agent"),
        P(),
        P(),
        P(None, None, "agent"),
        P(None, "agent", None),
    )
    return jax.shard_map(
        shards,
        mesh=mesh,
        in_specs=placed,
        out_specs=(P(None, None, None, "tile", "agent"), P(None, None, "tile", "agent")),
        check_vma=False,
    )
```

```python
import functools
import math

import jax
import jax.numpy as jnp
from jax import lax
from jax.experimental import pallas as pl
from jax.experimental.pallas import tpu as pltpu
from jax.sharding import PartitionSpec as P

PATCH = 16
LANES = 128
DENOM = 724.0


def split_pair(values):
    high = values.astype(jnp.bfloat16)
    low = (values - high.astype(jnp.float32)).astype(jnp.bfloat16)
    return high, low


def interpolation_rows(low_ref, frac_ref, angle, start, window):
    lows = low_ref[pl.ds(angle, 1), :] - start
    near = frac_ref[pl.ds(angle, 1), :].astype(jnp.float32) / DENOM
    far = 1.0 - near
    near_high = near.astype(jnp.bfloat16).astype(jnp.float32)
    far_high = far.astype(jnp.bfloat16).astype(jnp.float32)
    near_low, far_low = near - near_high, far - far_high
    apart = lax.broadcasted_iota(jnp.int32, (window, lows.shape[1]), 0) - lows
    at_near, at_far = apart == 0, apart == 1
    high = jnp.where(at_near, near_high, jnp.where(at_far, far_high, 0.0))
    low = jnp.where(at_near, near_low, jnp.where(at_far, far_low, 0.0))
    return jnp.concatenate([high.astype(jnp.bfloat16), low.astype(jnp.bfloat16)], axis=0)


def project_kernel(factor, window, starts_ref, volume_ref, low_ref, frac_ref, sino_ref):
    angles, planes, bins = sino_ref.shape
    high, low = split_pair(volume_ref[...])
    stacked = jnp.concatenate([high, low], axis=0)

    def step(angle, carry):
        start = starts_ref[angle]
        rows = interpolation_rows(low_ref, frac_ref, angle, start, window)
        out = lax.dot_general(
            stacked, rows, (((1,), (1,)), ((), ())), preferred_element_type=jnp.float32
        )
        out = out[:planes] + out[planes:]
        out = factor * (out[:, :window] + out[:, window:])
        if bins > window:
            out = jnp.concatenate([out, jnp.zeros((planes, bins - window), jnp.float32)], axis=1)
            out = pltpu.roll(out, start, 1)
        sino_ref[angle] = out
        return carry

    lax.fori_loop(0, angles, step, 0, unroll=4)


def spread_kernel(factor, window, starts_ref, misfit_ref, low_ref, frac_ref, volume_ref, out_ref):
    angles, planes, bins = misfit_ref.shape
    out_ref[...] = volume_ref[...]

    def step(angle, carry):
        start = starts_ref[angle]
        rows = interpolation_rows(low_ref, frac_ref, angle, start, window)
        resid = misfit_ref[angle]
        if bins > window:
            resid = pltpu.roll(resid, bins - start, 1)[:, :window]
        high, low = split_pair(resid)
        left = jnp.concatenate([high, low], axis=0)
        left = jnp.concatenate([left, left], axis=1)
        out = jnp.dot(left, rows, preferred_element_type=jnp.float32)
        out_ref[...] -= factor * (out[:planes] + out[planes:])
        return carry

    lax.fori_loop(0, angles, step, 0, unroll=4)


def exchange_kernel(
    chunks_ref, target_ref, patches_ref, up_ref, down_ref, misfit_ref, nets_ref,
    tile_parts, band, agent_parts, every, wide, terms, term_parts,
    tile_send, tile_recv, sum_send, sum_recv, own_send, own_recv,
    every_send, every_recv, patch_send, patch_recv, term_send, term_recv,
):
    tiles, agents = chunks_ref.shape[0], chunks_ref.shape[1]
    tile, agent = lax.axis_index("tile"), lax.axis_index("agent")

    def tile_at(step):
        return lax.rem(tile + step, tiles)

    def agent_at(step):
        return lax.rem(agent + step, agents)

    def copy(source, target, send, recv, step, to):
        return pltpu.make_async_remote_copy(
            src_ref=source,
            dst_ref=target,
            send_sem=send.at[step],
            recv_sem=recv.at[step],
            device_id=to,
            device_id_type=pl.DeviceIdType.MESH,
        )

    def to_tile(step):
        return (tile_at(step), agent)

    def to_agent(step):
        return (tile, agent_at(step))

    def over(count, body):
        def step_body(step, carry):
            body(step)
            return carry

        lax.fori_loop(1, count, step_body, 0)

    barrier = pltpu.get_barrier_semaphore()
    over(agents, lambda step: pl.semaphore_signal(
        barrier, inc=1, device_id=to_agent(step), device_id_type=pl.DeviceIdType.MESH))
    over(tiles, lambda step: pl.semaphore_signal(
        barrier, inc=1, device_id=to_tile(step), device_id_type=pl.DeviceIdType.MESH))
    pl.semaphore_wait(barrier, tiles + agents - 2)

    def tile_copy(step):
        return copy(
            chunks_ref.at[tile_at(step)], tile_parts.at[step], tile_send, tile_recv, step,
            to_tile(step))

    def patch_copy(which):
        return lambda step: copy(
            patches_ref.at[which], wide.at[which, step], patch_send.at[which],
            patch_recv.at[which], step, to_agent(step))

    def sum_copy(step):
        return copy(
            band.at[agent_at(step)], agent_parts.at[step], sum_send, sum_recv, step,
            to_agent(step))

    def own_copy(step):
        return copy(
            every.at[tile, agent], every.at[tile, agent], own_send, own_recv, step,
            to_agent(step))

    def own_arrival(step):
        where = every.at[tile, agent_at(agents - step)]
        return copy(where, where, own_send, own_recv, step, to_agent(step))

    def every_copy(step):
        return copy(
            every.at[tile], every.at[tile], every_send, every_recv, step, to_tile(step))

    def every_arrival(step):
        where = every.at[tile_at(tiles - step)]
        return copy(where, where, every_send, every_recv, step, to_tile(step))

    def term_copy(which):
        return lambda step: copy(
            terms.at[which, agents - step], term_parts.at[which, step], term_send.at[which],
            term_recv.at[which], step, to_agent(step))

    nets = range(patches_ref.shape[0])
    over(tiles, lambda step: tile_copy(step).start())
    for which in nets:
        over(agents, lambda step: patch_copy(which)(step).start())
        wide[which, 0] = patches_ref[which]
    band[...] = chunks_ref[tile]

    def add_tile(step):
        tile_copy(step).wait_recv()
        band[...] += tile_parts[step]

    over(tiles, add_tile)
    over(agents, lambda step: sum_copy(step).start())
    every[tile, agent] = band[agent] - target_ref[...]

    def add_agent(step):
        sum_copy(step).wait_recv()
        every[tile, agent] += agent_parts[step]

    over(agents, add_agent)
    over(agents, lambda step: own_copy(step).start())

    count = patches_ref.shape[1]
    for which in nets:
        over(agents, lambda step: patch_copy(which)(step).wait_recv())
        rows = wide[which].reshape(agents * count, patches_ref.shape[2])
        hidden = jnp.dot(rows, up_ref[which], preferred_element_type=jnp.float32)
        hidden = jnp.maximum(hidden, 0.0).astype(jnp.bfloat16)
        out = jnp.dot(hidden, down_ref[which], preferred_element_type=jnp.float32)
        terms[which] = out.reshape(agents, count, out.shape[1])
        over(agents, lambda step: term_copy(which)(step).start())

    over(agents, lambda step: own_arrival(step).wait_recv())
    over(tiles, lambda step: every_copy(step).start())
    over(tiles, lambda step: every_arrival(step).wait_recv())
    misfit_ref[...] = every[...]
    for which in nets:
        nets_ref[which] = terms[which, 0]

        def add_terms(step):
            term_copy(which)(step).wait_recv()
            nets_ref[which] += term_parts[which, step]

        over(agents, add_terms)
    over(tiles, lambda step: tile_copy(step).wait_send())
    for which in nets:
        over(agents, lambda step: patch_copy(which)(step).wait_send())
        over(agents, lambda step: term_copy(which)(step).wait_send())
    over(agents, lambda step: sum_copy(step).wait_send())
    over(agents, lambda step: own_copy(step).wait_send())
    over(tiles, lambda step: every_copy(step).wait_send())


def exchange(chunks, target, patches, up_weight, down_weight):
    tiles, agents, planes, own = chunks.shape
    whole = pl.BlockSpec(memory_space=pltpu.VMEM)
    nets = jax.ShapeDtypeStruct(patches.shape, jnp.float32)
    sems = [pltpu.SemaphoreType.DMA((n,)) for n in (
        tiles, tiles, agents, agents, agents, agents, tiles, tiles)]
    sems += [pltpu.SemaphoreType.DMA((patches.shape[0], agents))] * 4
    by_net = (patches.shape[0], agents) + patches.shape[1:]
    return pl.pallas_call(
        exchange_kernel,
        out_shape=(jax.ShapeDtypeStruct(chunks.shape, jnp.float32), nets),
        in_specs=[whole] * 5,
        out_specs=(whole, whole),
        scratch_shapes=[
            pltpu.VMEM(chunks.shape, jnp.float32),
            pltpu.VMEM((agents, planes, own), jnp.float32),
            pltpu.VMEM((agents, planes, own), jnp.float32),
            pltpu.VMEM(chunks.shape, jnp.float32),
            pltpu.VMEM(by_net, jnp.bfloat16),
            pltpu.VMEM(by_net, jnp.float32),
            pltpu.VMEM(by_net, jnp.float32),
            *sems,
        ],
        compiler_params=pltpu.CompilerParams(
            collective_id=0, has_side_effects=True, vmem_limit_bytes=48 * 2**20
        ),
        name="exchange",
    )(chunks, target, patches, up_weight, down_weight)


def permute(block, step_tile, step_agent):
    tiles, agents = lax.axis_size("tile"), lax.axis_size("agent")
    pairs = []
    for tile in range(tiles):
        for agent in range(agents):
            source = (tile + step_tile) % tiles * agents + (agent + step_agent) % agents
            pairs.append((source, tile * agents + agent))
    return lax.ppermute(block, ("tile", "agent"), pairs)


def pad_lanes(block):
    short = -block.shape[-1] % LANES
    return jnp.pad(block, ((0, 0),) * (block.ndim - 1) + ((0, short),))


def ahead_kernel(offsets_ref, both_ref, rows_ref, cols_ref, out_ref):
    planes, rows, cols = out_ref.shape[1:]

    def ahead(block, shift, axis):
        return pltpu.roll(block, block.shape[axis] - shift, axis)

    first = ahead(both_ref[...], offsets_ref[0], 1)[:, :rows]
    first = ahead(first, offsets_ref[0], 2)
    second = ahead(rows_ref[...], offsets_ref[1], 1)
    third = ahead(cols_ref[...], offsets_ref[2], 2)
    out_ref[0] = first[:, :, :cols].astype(out_ref.dtype)
    out_ref[1] = second[:, :rows, :cols].astype(out_ref.dtype)
    out_ref[2] = third[:, :, :cols].astype(out_ref.dtype)


def make_patches(noisy, offsets):
    times, slices, rows, cols = noisy.shape[1:]
    row_blocks, col_blocks = rows // PATCH, cols // PATCH
    flat = noisy.reshape(3, times * slices, rows, cols)
    below = permute(flat[:2, :, :PATCH], 1, 0)
    sides = jnp.stack([flat[0, :, :, :PATCH], flat[2, :, :, :PATCH]])
    beyond = permute(sides, 0, 1)
    corner = permute(flat[0, :, :PATCH, :PATCH], 1, 1)
    top = jnp.concatenate([flat[0], beyond[0]], axis=2)
    bottom = jnp.concatenate([below[0], corner], axis=2)
    both = pad_lanes(jnp.concatenate([top, bottom], axis=1).astype(jnp.float32))
    tall = pad_lanes(jnp.concatenate([flat[1], below[1]], axis=1).astype(jnp.float32))
    broad = pad_lanes(jnp.concatenate([flat[2], beyond[1]], axis=2).astype(jnp.float32))
    vmem = pl.BlockSpec(memory_space=pltpu.VMEM)
    moved = pl.pallas_call(
        ahead_kernel,
        out_shape=jax.ShapeDtypeStruct(flat.shape, jnp.bfloat16),
        in_specs=[pl.BlockSpec(memory_space=pltpu.SMEM), vmem, vmem, vmem],
        out_specs=vmem,
        compiler_params=pltpu.CompilerParams(vmem_limit_bytes=32 * 2**20),
        name="ahead",
    )(offsets, both, tall, broad)
    first = moved[0].reshape(times, slices, row_blocks, PATCH, col_blocks, PATCH)
    first = first.transpose(0, 1, 2, 4, 3, 5).reshape(-1, PATCH * PATCH)
    second = moved[1].reshape(times, slices, row_blocks, PATCH, cols)
    second = second.transpose(0, 2, 4, 1, 3).reshape(-1, slices * PATCH)
    third = moved[2].reshape(times, slices, rows, col_blocks, PATCH)
    third = third.transpose(0, 2, 3, 1, 4).reshape(-1, slices * PATCH)
    return jnp.stack([first, second, third])


def join_kernel(offsets_ref, weights_ref, state_ref, fit_ref, both_ref, rows_ref, cols_ref, out_ref):
    planes, rows, cols = fit_ref.shape

    def back(block, shift, axis):
        return pltpu.roll(block, block.shape[axis] - (PATCH - shift), axis)

    first = back(both_ref[...], offsets_ref[0], 1)[:, :rows]
    first = back(first, offsets_ref[0], 2)[:, :, :cols]
    second = back(rows_ref[...], offsets_ref[1], 1)[:, :rows, :cols]
    third = back(cols_ref[...], offsets_ref[2], 2)[:, :, :cols]
    answers = [fit_ref[...]]
    for which, removed in enumerate((first, second, third)):
        answers.append(state_ref[which + 1] - removed)
    total = weights_ref[0]
    for which in range(1, len(answers)):
        total = total + weights_ref[which]
    joined = jnp.zeros_like(answers[0])
    for which, answer in enumerate(answers):
        share = jnp.full(joined.shape, weights_ref[which]) / jnp.full(joined.shape, total)
        joined = joined + share * (2.0 * answer - state_ref[which])
    for which, answer in enumerate(answers):
        out_ref[which] = state_ref[which] + joined - answer


def spread_nets(nets, shape):
    times, slices, rows, cols = shape
    row_blocks, col_blocks = rows // PATCH, cols // PATCH
    flat = (times * slices, rows, cols)
    first = nets[0].reshape(times, slices, row_blocks, col_blocks, PATCH, PATCH)
    first = first.transpose(0, 1, 2, 4, 3, 5).reshape(flat)
    second = nets[1].reshape(times, row_blocks, cols, slices, PATCH)
    second = second.transpose(0, 3, 1, 4, 2).reshape(flat)
    third = nets[2].reshape(times, rows, col_blocks, slices, PATCH)
    third = third.transpose(0, 3, 1, 2, 4).reshape(flat)
    low_row, low_col = rows - PATCH, cols - PATCH
    above = permute(jnp.stack([first[:, low_row:], second[:, low_row:]]), -1, 0)
    before = permute(jnp.stack([first[:, :, low_col:], third[:, :, low_col:]]), 0, -1)
    corner = permute(first[:, low_row:, low_col:], -1, -1)
    top = jnp.concatenate([corner, above[0]], axis=2)
    bottom = jnp.concatenate([before[0], first], axis=2)
    both = pad_lanes(jnp.concatenate([top, bottom], axis=1))
    tall = pad_lanes(jnp.concatenate([above[1], second], axis=1))
    broad = pad_lanes(jnp.concatenate([before[1], third], axis=2))
    return both, tall, broad


def join(offsets, weights, state, data_fit, both, tall, broad):
    agents, times, slices, rows, cols = state.shape
    vmem = pl.BlockSpec(memory_space=pltpu.VMEM)
    smem = pl.BlockSpec(memory_space=pltpu.SMEM)
    flat = state.reshape(agents, times * slices, rows, cols)
    out = pl.pallas_call(
        join_kernel,
        out_shape=jax.ShapeDtypeStruct(flat.shape, jnp.float32),
        in_specs=[smem, smem, vmem, vmem, vmem, vmem, vmem],
        out_specs=vmem,
        compiler_params=pltpu.CompilerParams(vmem_limit_bytes=32 * 2**20),
        name="join",
    )(offsets, weights, flat, data_fit.reshape(flat.shape[1:]), both, tall, broad)
    return out.reshape(state.shape)


def data_and_nets(
    volume, bin_index, bin_frac, measured, factor, patches, up_weight, down_weight
):
    angles = bin_index.shape[0]
    planes = volume.shape[0] * volume.shape[1]
    current = volume.reshape(planes, -1)
    tiles, agents, own = lax.axis_size("tile"), lax.axis_size("agent"), measured.shape[2]
    bins = tiles * agents * own // angles
    window = -(-(bin_index.shape[1] + bin_index.shape[2] + 2) // LANES) * LANES
    window = min(window, bins)
    lows = bin_index.reshape(angles, -1)
    fracs = bin_frac.reshape(angles, -1)
    corners = bin_index[:, :: bin_index.shape[1] - 1, :: bin_index.shape[2] - 1]
    starts = jnp.minimum(jnp.min(corners, axis=(1, 2)), bins - window)
    whole = pl.BlockSpec(memory_space=pltpu.VMEM)
    scalars = pl.BlockSpec(memory_space=pltpu.SMEM)
    cost = pl.CostEstimate(
        flops=4 * angles * window * current.shape[1] * planes * 2,
        bytes_accessed=3 * current.size * 4,
        transcendentals=0,
    )
    grant = pltpu.CompilerParams(vmem_limit_bytes=48 * 2**20)
    sino = pl.pallas_call(
        functools.partial(project_kernel, factor, window),
        out_shape=jax.ShapeDtypeStruct((angles, planes, bins), jnp.float32),
        in_specs=[scalars, whole, whole, whole],
        out_specs=whole,
        cost_estimate=cost,
        compiler_params=grant,
        name="project",
    )(starts, current, lows, fracs)
    chunks = jnp.transpose(sino, (1, 0, 2)).reshape(planes, tiles, agents, own)
    chunks = jnp.transpose(chunks, (1, 2, 0, 3))
    misfit, nets = exchange(
        chunks, measured.reshape(planes, own), patches, up_weight, down_weight
    )
    by_angle = jnp.transpose(misfit, (2, 0, 1, 3)).reshape(planes, angles, bins)
    by_angle = jnp.transpose(by_angle, (1, 0, 2))
    result = pl.pallas_call(
        functools.partial(spread_kernel, factor, window),
        out_shape=jax.ShapeDtypeStruct(current.shape, jnp.float32),
        in_specs=[scalars, whole, whole, whole, whole],
        out_specs=whole,
        cost_estimate=cost,
        compiler_params=grant,
        name="spread",
    )(starts, by_angle, lows, fracs, current)
    return result.reshape(volume.shape), nets


def shards(
    agent_state, measured, bin_index, bin_frac, patch_offsets, agent_weights, up_weight, down_weight
):
    row_count = agent_state.shape[3]
    col_count = agent_state.shape[4]
    tile_count = lax.axis_size("tile")
    agent_count = lax.axis_size("agent")
    full_rows = row_count * tile_count
    full_cols = col_count * agent_count
    angles = bin_index.shape[0]
    factor = 1.0 / math.sqrt(angles * (full_rows + full_cols))
    patches = make_patches(agent_state[1:].astype(jnp.bfloat16), patch_offsets)
    data_fit, nets = data_and_nets(
        agent_state[0], bin_index, bin_frac, measured, factor, patches, up_weight, down_weight
    )
    parts = spread_nets(nets, agent_state.shape[1:])
    state_next = join(patch_offsets, agent_weights, agent_state, data_fit, *parts)
    return (state_next, data_fit)


def solution(mesh):
    placed = (
        P(None, None, None, "tile", "agent"),
        P(None, None, ("tile", "agent")),
        P(None, "tile", "agent"),
        P(None, "tile", "agent"),
        P(),
        P(),
        P(None, None, "agent"),
        P(None, "agent", None),
    )
    return jax.shard_map(
        shards,
        mesh=mesh,
        in_specs=placed,
        out_specs=(P(None, None, None, "tile", "agent"), P(None, None, "tile", "agent")),
        check_vma=False,
    )
```

```python
import functools
import math

import jax
import jax.numpy as jnp
from jax import lax
from jax.experimental import pallas as pl
from jax.experimental.pallas import tpu as pltpu
from jax.sharding import PartitionSpec as P

PATCH = 16
LANES = 128
DENOM = 724.0


def split_pair(values):
    high = values.astype(jnp.bfloat16)
    low = (values - high.astype(jnp.float32)).astype(jnp.bfloat16)
    return high, low


def interpolation_rows(low_ref, frac_ref, angle, start, window):
    lows = low_ref[pl.ds(angle, 1), :] - start
    near = frac_ref[pl.ds(angle, 1), :].astype(jnp.float32) / DENOM
    far = 1.0 - near
    near_high = near.astype(jnp.bfloat16).astype(jnp.float32)
    far_high = far.astype(jnp.bfloat16).astype(jnp.float32)
    near_low, far_low = near - near_high, far - far_high
    apart = lax.broadcasted_iota(jnp.int32, (window, lows.shape[1]), 0) - lows
    at_near, at_far = apart == 0, apart == 1
    high = jnp.where(at_near, near_high, jnp.where(at_far, far_high, 0.0))
    low = jnp.where(at_near, near_low, jnp.where(at_far, far_low, 0.0))
    return jnp.concatenate([high.astype(jnp.bfloat16), low.astype(jnp.bfloat16)], axis=0)


def project_kernel(factor, window, starts_ref, volume_ref, low_ref, frac_ref, sino_ref):
    angles, planes, bins = sino_ref.shape
    high, low = split_pair(volume_ref[...])
    stacked = jnp.concatenate([high, low], axis=0)

    def step(angle, carry):
        start = starts_ref[angle]
        rows = interpolation_rows(low_ref, frac_ref, angle, start, window)
        out = lax.dot_general(
            stacked, rows, (((1,), (1,)), ((), ())), preferred_element_type=jnp.float32
        )
        out = out[:planes] + out[planes:]
        out = factor * (out[:, :window] + out[:, window:])
        if bins > window:
            out = jnp.concatenate([out, jnp.zeros((planes, bins - window), jnp.float32)], axis=1)
            out = pltpu.roll(out, start, 1)
        sino_ref[angle] = out
        return carry

    lax.fori_loop(0, angles, step, 0, unroll=4)


def spread_kernel(factor, window, starts_ref, misfit_ref, low_ref, frac_ref, volume_ref, out_ref):
    angles, planes, bins = misfit_ref.shape
    out_ref[...] = volume_ref[...]

    def step(angle, carry):
        start = starts_ref[angle]
        rows = interpolation_rows(low_ref, frac_ref, angle, start, window)
        resid = misfit_ref[angle]
        if bins > window:
            resid = pltpu.roll(resid, bins - start, 1)[:, :window]
        high, low = split_pair(resid)
        left = jnp.concatenate([high, low], axis=0)
        left = jnp.concatenate([left, left], axis=1)
        out = jnp.dot(left, rows, preferred_element_type=jnp.float32)
        out_ref[...] -= factor * (out[:planes] + out[planes:])
        return carry

    lax.fori_loop(0, angles, step, 0, unroll=4)


def exchange_kernel(
    chunks_ref, target_ref, patches_ref, up_ref, down_ref,
    misfit_ref, both_ref, rows_ref, cols_ref,
    tile_parts, band, agent_parts, every, wide, terms, term_parts,
    tile_send, tile_recv, sum_send, sum_recv, own_send, own_recv,
    every_send, every_recv, patch_send, patch_recv, term_send, term_recv,
    edge_send, edge_recv,
):
    tiles, agents = chunks_ref.shape[0], chunks_ref.shape[1]
    tile, agent = lax.axis_index("tile"), lax.axis_index("agent")

    def tile_at(step):
        return lax.rem(tile + step, tiles)

    def agent_at(step):
        return lax.rem(agent + step, agents)

    def copy(source, target, send, recv, step, to):
        return pltpu.make_async_remote_copy(
            src_ref=source,
            dst_ref=target,
            send_sem=send.at[step],
            recv_sem=recv.at[step],
            device_id=to,
            device_id_type=pl.DeviceIdType.MESH,
        )

    def to_tile(step):
        return (tile_at(step), agent)

    def to_agent(step):
        return (tile, agent_at(step))

    def over(count, body):
        def step_body(step, carry):
            body(step)
            return carry

        lax.fori_loop(1, count, step_body, 0)

    barrier = pltpu.get_barrier_semaphore()
    over(agents, lambda step: pl.semaphore_signal(
        barrier, inc=1, device_id=to_agent(step), device_id_type=pl.DeviceIdType.MESH))
    over(tiles, lambda step: pl.semaphore_signal(
        barrier, inc=1, device_id=to_tile(step), device_id_type=pl.DeviceIdType.MESH))
    pl.semaphore_signal(
        barrier, inc=1, device_id=(tile_at(tiles - 1), agent_at(agents - 1)),
        device_id_type=pl.DeviceIdType.MESH)
    pl.semaphore_wait(barrier, tiles + agents - 1)

    def tile_copy(step):
        return copy(
            chunks_ref.at[tile_at(step)], tile_parts.at[step], tile_send, tile_recv, step,
            to_tile(step))

    def patch_copy(which):
        return lambda step: copy(
            patches_ref.at[which], wide.at[which, step], patch_send.at[which],
            patch_recv.at[which], step, to_agent(step))

    def sum_copy(step):
        return copy(
            band.at[agent_at(step)], agent_parts.at[step], sum_send, sum_recv, step,
            to_agent(step))

    def own_copy(step):
        return copy(
            every.at[tile, agent], every.at[tile, agent], own_send, own_recv, step,
            to_agent(step))

    def own_arrival(step):
        where = every.at[tile, agent_at(agents - step)]
        return copy(where, where, own_send, own_recv, step, to_agent(step))

    def every_copy(step):
        return copy(
            every.at[tile], every.at[tile], every_send, every_recv, step, to_tile(step))

    def every_arrival(step):
        where = every.at[tile_at(tiles - step)]
        return copy(where, where, every_send, every_recv, step, to_tile(step))

    def term_copy(which):
        return lambda step: copy(
            terms.at[which, agents - step], term_parts.at[which, step], term_send.at[which],
            term_recv.at[which], step, to_agent(step))

    nets = range(patches_ref.shape[0])
    over(tiles, lambda step: tile_copy(step).start())
    for which in nets:
        over(agents, lambda step: patch_copy(which)(step).start())
        wide[which, 0] = patches_ref[which]
    band[...] = chunks_ref[tile]

    def add_tile(step):
        tile_copy(step).wait_recv()
        band[...] += tile_parts[step]

    over(tiles, add_tile)
    over(agents, lambda step: sum_copy(step).start())
    every[tile, agent] = band[agent] - target_ref[...]

    def add_agent(step):
        sum_copy(step).wait_recv()
        every[tile, agent] += agent_parts[step]

    over(agents, add_agent)
    over(agents, lambda step: own_copy(step).start())

    count = patches_ref.shape[1]
    for which in nets:
        over(agents, lambda step: patch_copy(which)(step).wait_recv())
        rows = wide[which].reshape(agents * count, patches_ref.shape[2])
        hidden = jnp.dot(rows, up_ref[which], preferred_element_type=jnp.float32)
        hidden = jnp.maximum(hidden, 0.0).astype(jnp.bfloat16)
        out = jnp.dot(hidden, down_ref[which], preferred_element_type=jnp.float32)
        terms[which] = out.reshape(agents, count, out.shape[1])
        over(agents, lambda step: term_copy(which)(step).start())

    over(agents, lambda step: own_arrival(step).wait_recv())
    over(tiles, lambda step: every_copy(step).start())
    over(tiles, lambda step: every_arrival(step).wait_recv())
    misfit_ref[...] = every[...]
    row_blocks, col_blocks = both_ref.shape[0] - 1, both_ref.shape[1] - 1
    next_tile, next_agent = to_tile(1), to_agent(1)
    across = (next_tile[0], next_agent[1])
    inner_rows, inner_cols = pl.ds(1, row_blocks), pl.ds(1, col_blocks)
    edges = (
        (
            (both_ref.at[row_blocks, inner_cols], both_ref.at[0, inner_cols], 0, next_tile),
            (both_ref.at[inner_rows, col_blocks], both_ref.at[inner_rows, 0], 1, next_agent),
            (both_ref.at[row_blocks, col_blocks], both_ref.at[0, 0], 2, across),
        ),
        ((rows_ref.at[row_blocks], rows_ref.at[0], 3, next_tile),),
        ((cols_ref.at[col_blocks], cols_ref.at[0], 4, next_agent),),
    )

    def edge_copies(which):
        return [copy(source, target, edge_send, edge_recv, step, to)
                for source, target, step, to in edges[which]]

    for which in nets:

        def add_terms(step):
            term_copy(which)(step).wait_recv()
            terms[which, 0] += term_parts[which, step]

        over(agents, add_terms)
        total = terms[which, 0]
        if which == 0:
            both_ref[1:, 1:] = total.reshape((row_blocks, col_blocks) + both_ref.shape[2:])
        elif which == 1:
            rows_ref[1:] = total.reshape((row_blocks,) + rows_ref.shape[1:])
        else:
            cols_ref[1:] = total.reshape((col_blocks,) + cols_ref.shape[1:])
        for edge in edge_copies(which):
            edge.start()
    for which in nets:
        for edge in edge_copies(which):
            edge.wait()
    over(tiles, lambda step: tile_copy(step).wait_send())
    for which in nets:
        over(agents, lambda step: patch_copy(which)(step).wait_send())
        over(agents, lambda step: term_copy(which)(step).wait_send())
    over(agents, lambda step: sum_copy(step).wait_send())
    over(agents, lambda step: own_copy(step).wait_send())
    over(tiles, lambda step: every_copy(step).wait_send())


def exchange(chunks, target, patches, up_weight, down_weight, row_blocks, col_blocks):
    tiles, agents, planes, own = chunks.shape
    whole = pl.BlockSpec(memory_space=pltpu.VMEM)
    count, pixels = patches.shape[1:]
    shapes = (
        (row_blocks + 1, col_blocks + 1, count // (row_blocks * col_blocks), pixels),
        (row_blocks + 1, count // row_blocks, pixels),
        (col_blocks + 1, count // col_blocks, pixels),
    )
    parts = tuple(jax.ShapeDtypeStruct(shape, jnp.float32) for shape in shapes)
    sems = [pltpu.SemaphoreType.DMA((n,)) for n in (
        tiles, tiles, agents, agents, agents, agents, tiles, tiles)]
    sems += [pltpu.SemaphoreType.DMA((patches.shape[0], agents))] * 4
    sems += [pltpu.SemaphoreType.DMA((5,))] * 2
    by_net = (patches.shape[0], agents) + patches.shape[1:]
    return pl.pallas_call(
        exchange_kernel,
        out_shape=(jax.ShapeDtypeStruct(chunks.shape, jnp.float32),) + parts,
        in_specs=[whole] * 5,
        out_specs=(whole,) * 4,
        scratch_shapes=[
            pltpu.VMEM(chunks.shape, jnp.float32),
            pltpu.VMEM((agents, planes, own), jnp.float32),
            pltpu.VMEM((agents, planes, own), jnp.float32),
            pltpu.VMEM(chunks.shape, jnp.float32),
            pltpu.VMEM(by_net, jnp.bfloat16),
            pltpu.VMEM(by_net, jnp.float32),
            pltpu.VMEM(by_net, jnp.float32),
            *sems,
        ],
        compiler_params=pltpu.CompilerParams(
            collective_id=0, has_side_effects=True, vmem_limit_bytes=48 * 2**20
        ),
        name="exchange",
    )(chunks, target, patches, up_weight, down_weight)


def permute(block, step_tile, step_agent):
    tiles, agents = lax.axis_size("tile"), lax.axis_size("agent")
    pairs = []
    for tile in range(tiles):
        for agent in range(agents):
            source = (tile + step_tile) % tiles * agents + (agent + step_agent) % agents
            pairs.append((source, tile * agents + agent))
    return lax.ppermute(block, ("tile", "agent"), pairs)


def pad_lanes(block):
    short = -block.shape[-1] % LANES
    return jnp.pad(block, ((0, 0),) * (block.ndim - 1) + ((0, short),))


def ahead_kernel(offsets_ref, both_ref, rows_ref, cols_ref, out_ref):
    planes, rows, cols = out_ref.shape[1:]

    def ahead(block, shift, axis):
        return pltpu.roll(block, block.shape[axis] - shift, axis)

    first = ahead(both_ref[...], offsets_ref[0], 1)[:, :rows]
    first = ahead(first, offsets_ref[0], 2)
    second = ahead(rows_ref[...], offsets_ref[1], 1)
    third = ahead(cols_ref[...], offsets_ref[2], 2)
    out_ref[0] = first[:, :, :cols].astype(out_ref.dtype)
    out_ref[1] = second[:, :rows, :cols].astype(out_ref.dtype)
    out_ref[2] = third[:, :, :cols].astype(out_ref.dtype)


def make_patches(noisy, offsets):
    times, slices, rows, cols = noisy.shape[1:]
    row_blocks, col_blocks = rows // PATCH, cols // PATCH
    flat = noisy.reshape(3, times * slices, rows, cols)
    below = permute(flat[:2, :, :PATCH], 1, 0)
    sides = jnp.stack([flat[0, :, :, :PATCH], flat[2, :, :, :PATCH]])
    beyond = permute(sides, 0, 1)
    corner = permute(flat[0, :, :PATCH, :PATCH], 1, 1)
    top = jnp.concatenate([flat[0], beyond[0]], axis=2)
    bottom = jnp.concatenate([below[0], corner], axis=2)
    both = pad_lanes(jnp.concatenate([top, bottom], axis=1).astype(jnp.float32))
    tall = pad_lanes(jnp.concatenate([flat[1], below[1]], axis=1).astype(jnp.float32))
    broad = pad_lanes(jnp.concatenate([flat[2], beyond[1]], axis=2).astype(jnp.float32))
    vmem = pl.BlockSpec(memory_space=pltpu.VMEM)
    moved = pl.pallas_call(
        ahead_kernel,
        out_shape=jax.ShapeDtypeStruct(flat.shape, jnp.float32),
        in_specs=[pl.BlockSpec(memory_space=pltpu.SMEM), vmem, vmem, vmem],
        out_specs=vmem,
        compiler_params=pltpu.CompilerParams(vmem_limit_bytes=32 * 2**20),
        name="ahead",
    )(offsets, both, tall, broad)
    first = moved[0].reshape(times * slices, row_blocks, PATCH, col_blocks, PATCH)
    first = first.transpose(1, 3, 0, 2, 4).reshape(-1, PATCH * PATCH)
    second = moved[1].reshape(times, slices, row_blocks, PATCH, cols)
    second = second.transpose(2, 0, 4, 1, 3).reshape(-1, slices * PATCH)
    third = moved[2].reshape(times, slices, rows, col_blocks, PATCH)
    third = third.transpose(3, 0, 2, 1, 4).reshape(-1, slices * PATCH)
    return jnp.stack([first, second, third]).astype(jnp.bfloat16)


def join_kernel(offsets_ref, weights_ref, state_ref, fit_ref, both_ref, rows_ref, cols_ref, out_ref):
    planes, rows, cols = fit_ref.shape

    def back(block, shift, axis):
        return pltpu.roll(block, block.shape[axis] - (PATCH - shift), axis)

    first = back(both_ref[...], offsets_ref[0], 1)[:, :rows]
    first = back(first, offsets_ref[0], 2)[:, :, :cols]
    second = back(rows_ref[...], offsets_ref[1], 1)[:, :rows, :cols]
    third = back(cols_ref[...], offsets_ref[2], 2)[:, :, :cols]
    answers = [fit_ref[...]]
    for which, removed in enumerate((first, second, third)):
        answers.append(state_ref[which + 1] - removed)
    total = weights_ref[0]
    for which in range(1, len(answers)):
        total = total + weights_ref[which]
    joined = jnp.zeros_like(answers[0])
    for which, answer in enumerate(answers):
        share = jnp.full(joined.shape, weights_ref[which]) / jnp.full(joined.shape, total)
        joined = joined + share * (2.0 * answer - state_ref[which])
    for which, answer in enumerate(answers):
        out_ref[which] = state_ref[which] + joined - answer


def spread_nets(nets, shape):
    times, slices, rows, cols = shape
    planes = times * slices
    tall_blocks, broad_blocks = rows // PATCH + 1, cols // PATCH + 1
    both = nets[0].reshape(tall_blocks, broad_blocks, planes, PATCH, PATCH)
    both = both.transpose(2, 0, 3, 1, 4).reshape(planes, rows + PATCH, cols + PATCH)
    tall = nets[1].reshape(tall_blocks, times, cols, slices, PATCH)
    tall = tall.transpose(1, 3, 0, 4, 2).reshape(planes, rows + PATCH, cols)
    broad = nets[2].reshape(broad_blocks, times, rows, slices, PATCH)
    broad = broad.transpose(1, 3, 2, 0, 4).reshape(planes, rows, cols + PATCH)
    return pad_lanes(both), pad_lanes(tall), pad_lanes(broad)


def join(offsets, weights, state, data_fit, both, tall, broad):
    agents, times, slices, rows, cols = state.shape
    vmem = pl.BlockSpec(memory_space=pltpu.VMEM)
    smem = pl.BlockSpec(memory_space=pltpu.SMEM)
    flat = state.reshape(agents, times * slices, rows, cols)
    out = pl.pallas_call(
        join_kernel,
        out_shape=jax.ShapeDtypeStruct(flat.shape, jnp.float32),
        in_specs=[smem, smem, vmem, vmem, vmem, vmem, vmem],
        out_specs=vmem,
        compiler_params=pltpu.CompilerParams(vmem_limit_bytes=32 * 2**20),
        name="join",
    )(offsets, weights, flat, data_fit.reshape(flat.shape[1:]), both, tall, broad)
    return out.reshape(state.shape)


def data_and_nets(
    volume, bin_index, bin_frac, measured, factor, patches, up_weight, down_weight
):
    angles = bin_index.shape[0]
    planes = volume.shape[0] * volume.shape[1]
    current = volume.reshape(planes, -1)
    tiles, agents, own = lax.axis_size("tile"), lax.axis_size("agent"), measured.shape[2]
    bins = tiles * agents * own // angles
    window = -(-(bin_index.shape[1] + bin_index.shape[2] + 2) // LANES) * LANES
    window = min(window, bins)
    lows = bin_index.reshape(angles, -1)
    fracs = bin_frac.reshape(angles, -1)
    corners = bin_index[:, :: bin_index.shape[1] - 1, :: bin_index.shape[2] - 1]
    starts = jnp.minimum(jnp.min(corners, axis=(1, 2)), bins - window)
    whole = pl.BlockSpec(memory_space=pltpu.VMEM)
    scalars = pl.BlockSpec(memory_space=pltpu.SMEM)
    cost = pl.CostEstimate(
        flops=4 * angles * window * current.shape[1] * planes * 2,
        bytes_accessed=3 * current.size * 4,
        transcendentals=0,
    )
    grant = pltpu.CompilerParams(vmem_limit_bytes=48 * 2**20)
    sino = pl.pallas_call(
        functools.partial(project_kernel, factor, window),
        out_shape=jax.ShapeDtypeStruct((angles, planes, bins), jnp.float32),
        in_specs=[scalars, whole, whole, whole],
        out_specs=whole,
        cost_estimate=cost,
        compiler_params=grant,
        name="project",
    )(starts, current, lows, fracs)
    chunks = jnp.transpose(sino, (1, 0, 2)).reshape(planes, tiles, agents, own)
    chunks = jnp.transpose(chunks, (1, 2, 0, 3))
    misfit, *nets = exchange(
        chunks, measured.reshape(planes, own), patches, up_weight, down_weight,
        bin_index.shape[1] // PATCH, bin_index.shape[2] // PATCH,
    )
    by_angle = jnp.transpose(misfit, (2, 0, 1, 3)).reshape(planes, angles, bins)
    by_angle = jnp.transpose(by_angle, (1, 0, 2))
    result = pl.pallas_call(
        functools.partial(spread_kernel, factor, window),
        out_shape=jax.ShapeDtypeStruct(current.shape, jnp.float32),
        in_specs=[scalars, whole, whole, whole, whole],
        out_specs=whole,
        cost_estimate=cost,
        compiler_params=grant,
        name="spread",
    )(starts, by_angle, lows, fracs, current)
    return result.reshape(volume.shape), nets


def shards(
    agent_state, measured, bin_index, bin_frac, patch_offsets, agent_weights, up_weight, down_weight
):
    row_count = agent_state.shape[3]
    col_count = agent_state.shape[4]
    tile_count = lax.axis_size("tile")
    agent_count = lax.axis_size("agent")
    full_rows = row_count * tile_count
    full_cols = col_count * agent_count
    angles = bin_index.shape[0]
    factor = 1.0 / math.sqrt(angles * (full_rows + full_cols))
    patches = make_patches(agent_state[1:].astype(jnp.bfloat16), patch_offsets)
    data_fit, nets = data_and_nets(
        agent_state[0], bin_index, bin_frac, measured, factor, patches, up_weight, down_weight
    )
    parts = spread_nets(nets, agent_state.shape[1:])
    state_next = join(patch_offsets, agent_weights, agent_state, data_fit, *parts)
    return (state_next, data_fit)


def solution(mesh):
    placed = (
        P(None, None, None, "tile", "agent"),
        P(None, None, ("tile", "agent")),
        P(None, "tile", "agent"),
        P(None, "tile", "agent"),
        P(),
        P(),
        P(None, None, "agent"),
        P(None, "agent", None),
    )
    return jax.shard_map(
        shards,
        mesh=mesh,
        in_specs=placed,
        out_specs=(P(None, None, None, "tile", "agent"), P(None, None, "tile", "agent")),
        check_vma=False,
    )
```

```python
import functools
import math

import jax
import jax.numpy as jnp
from jax import lax
from jax.experimental import pallas as pl
from jax.experimental.pallas import tpu as pltpu
from jax.sharding import PartitionSpec as P

PATCH = 16
LANES = 128
DENOM = 724.0


def split_pair(values):
    high = values.astype(jnp.bfloat16)
    low = (values - high.astype(jnp.float32)).astype(jnp.bfloat16)
    return high, low


def interpolation_rows(low_ref, frac_ref, angle, start, window):
    lows = low_ref[pl.ds(angle, 1), :] - start
    near = frac_ref[pl.ds(angle, 1), :].astype(jnp.float32) / DENOM
    far = 1.0 - near
    near_high = near.astype(jnp.bfloat16).astype(jnp.float32)
    far_high = far.astype(jnp.bfloat16).astype(jnp.float32)
    near_low, far_low = near - near_high, far - far_high
    apart = lax.broadcasted_iota(jnp.int32, (window, lows.shape[1]), 0) - lows
    at_near, at_far = apart == 0, apart == 1
    high = jnp.where(at_near, near_high, jnp.where(at_far, far_high, 0.0))
    low = jnp.where(at_near, near_low, jnp.where(at_far, far_low, 0.0))
    return jnp.concatenate([high.astype(jnp.bfloat16), low.astype(jnp.bfloat16)], axis=0)


def project(factor, window, bins, starts_ref, volume_ref, low_ref, frac_ref, sino_ref):
    angles, (planes, own) = low_ref.shape[0], sino_ref.shape[1:]
    parts = bins // own
    high, low = split_pair(volume_ref[...])
    stacked = jnp.concatenate([high, low], axis=0)

    def step(angle, carry):
        start = starts_ref[angle]
        rows = interpolation_rows(low_ref, frac_ref, angle, start, window)
        out = lax.dot_general(
            stacked, rows, (((1,), (1,)), ((), ())), preferred_element_type=jnp.float32
        )
        out = out[:planes] + out[planes:]
        out = factor * (out[:, :window] + out[:, window:])
        if bins > window:
            out = jnp.concatenate([out, jnp.zeros((planes, bins - window), jnp.float32)], axis=1)
            out = pltpu.roll(out, start, 1)
        for part in range(parts):
            sino_ref[angle * parts + part] = out[:, part * own : (part + 1) * own]
        return carry

    lax.fori_loop(0, angles, step, 0, unroll=4)


def spread(factor, window, bins, starts_ref, misfit_ref, low_ref, frac_ref, volume_ref, out_ref):
    angles, (planes, own) = low_ref.shape[0], misfit_ref.shape[1:]
    parts = bins // own
    out_ref[...] = volume_ref[...]

    def step(angle, carry):
        start = starts_ref[angle]
        rows = interpolation_rows(low_ref, frac_ref, angle, start, window)
        resid = jnp.concatenate(
            [misfit_ref[angle * parts + part] for part in range(parts)], axis=1
        )
        if bins > window:
            resid = pltpu.roll(resid, bins - start, 1)[:, :window]
        high, low = split_pair(resid)
        left = jnp.concatenate([high, low], axis=0)
        left = jnp.concatenate([left, left], axis=1)
        out = jnp.dot(left, rows, preferred_element_type=jnp.float32)
        out_ref[...] -= factor * (out[:planes] + out[planes:])
        return carry

    lax.fori_loop(0, angles, step, 0, unroll=4)


def exchange_kernel(
    factor, window, bins, agents,
    starts_ref, volume_ref, low_ref, frac_ref, target_ref, patches_ref, up_ref, down_ref,
    fit_ref, both_ref, rows_ref, cols_ref,
    chunks, tile_parts, band, agent_parts, every, wide, terms, term_parts,
    tile_send, tile_recv, sum_send, sum_recv, own_send, own_recv,
    every_send, every_recv, patch_send, patch_recv, term_send, term_recv,
    edge_send, edge_recv,
):
    tiles = chunks.shape[0] // agents
    tile, agent = lax.axis_index("tile"), lax.axis_index("agent")
    mine = tile * agents + agent

    def tile_at(step):
        return lax.rem(tile + step, tiles)

    def agent_at(step):
        return lax.rem(agent + step, agents)

    def copy(source, target, send, recv, step, to):
        return pltpu.make_async_remote_copy(
            src_ref=source,
            dst_ref=target,
            send_sem=send.at[step],
            recv_sem=recv.at[step],
            device_id=to,
            device_id_type=pl.DeviceIdType.MESH,
        )

    def share_of(which):
        return pl.ds(which * agents, agents)

    def to_tile(step):
        return (tile_at(step), agent)

    def to_agent(step):
        return (tile, agent_at(step))

    def over(count, body):
        def step_body(step, carry):
            body(step)
            return carry

        lax.fori_loop(1, count, step_body, 0)

    barrier = pltpu.get_barrier_semaphore()
    over(agents, lambda step: pl.semaphore_signal(
        barrier, inc=1, device_id=to_agent(step), device_id_type=pl.DeviceIdType.MESH))
    over(tiles, lambda step: pl.semaphore_signal(
        barrier, inc=1, device_id=to_tile(step), device_id_type=pl.DeviceIdType.MESH))
    pl.semaphore_signal(
        barrier, inc=1, device_id=(tile_at(tiles - 1), agent_at(agents - 1)),
        device_id_type=pl.DeviceIdType.MESH)
    pl.semaphore_wait(barrier, tiles + agents - 1)

    def tile_copy(step):
        return copy(
            chunks.at[share_of(tile_at(step))], tile_parts.at[step], tile_send, tile_recv, step,
            to_tile(step))

    def patch_copy(which):
        return lambda step: copy(
            patches_ref.at[which], wide.at[which, step], patch_send.at[which],
            patch_recv.at[which], step, to_agent(step))

    def sum_copy(step):
        return copy(
            band.at[agent_at(step)], agent_parts.at[step], sum_send, sum_recv, step,
            to_agent(step))

    def own_copy(step):
        return copy(
            every.at[mine], every.at[mine], own_send, own_recv, step,
            to_agent(step))

    def own_arrival(step):
        where = every.at[tile * agents + agent_at(agents - step)]
        return copy(where, where, own_send, own_recv, step, to_agent(step))

    def every_copy(step):
        return copy(
            every.at[share_of(tile)], every.at[share_of(tile)], every_send, every_recv, step, to_tile(step))

    def every_arrival(step):
        where = every.at[share_of(tile_at(tiles - step))]
        return copy(where, where, every_send, every_recv, step, to_tile(step))

    def term_copy(which):
        return lambda step: copy(
            terms.at[which, agents - step], term_parts.at[which, step], term_send.at[which],
            term_recv.at[which], step, to_agent(step))

    nets = range(patches_ref.shape[0])
    count = patches_ref.shape[1]

    def run_net(which):
        over(agents, lambda step: patch_copy(which)(step).wait_recv())
        rows = wide[which].reshape(agents * count, patches_ref.shape[2])
        hidden = jnp.dot(rows, up_ref[which], preferred_element_type=jnp.float32)
        hidden = jnp.maximum(hidden, 0.0).astype(jnp.bfloat16)
        out = jnp.dot(hidden, down_ref[which], preferred_element_type=jnp.float32)
        terms[which] = out.reshape(agents, count, out.shape[1])
        over(agents, lambda step: term_copy(which)(step).start())

    def add_tile(step):
        tile_copy(step).wait_recv()
        band[...] += tile_parts[step]

    def add_agent(step):
        sum_copy(step).wait_recv()
        every[mine] += agent_parts[step]

    for which in nets:
        over(agents, lambda step: patch_copy(which)(step).start())
        wide[which, 0] = patches_ref[which]
    project(factor, window, bins, starts_ref, volume_ref, low_ref, frac_ref, chunks)
    over(tiles, lambda step: tile_copy(step).start())
    band[...] = chunks[share_of(tile)]
    run_net(0)
    over(tiles, add_tile)
    over(agents, lambda step: sum_copy(step).start())
    every[mine] = band[agent] - target_ref[...]
    run_net(1)
    over(agents, add_agent)
    over(agents, lambda step: own_copy(step).start())
    run_net(2)
    over(agents, lambda step: own_arrival(step).wait_recv())
    over(tiles, lambda step: every_copy(step).start())
    over(tiles, lambda step: every_arrival(step).wait_recv())
    spread(factor, window, bins, starts_ref, every, low_ref, frac_ref, volume_ref, fit_ref)
    row_blocks, col_blocks = both_ref.shape[0] - 1, both_ref.shape[1] - 1
    next_tile, next_agent = to_tile(1), to_agent(1)
    across = (next_tile[0], next_agent[1])
    inner_rows, inner_cols = pl.ds(1, row_blocks), pl.ds(1, col_blocks)
    edges = (
        (
            (both_ref.at[row_blocks, inner_cols], both_ref.at[0, inner_cols], 0, next_tile),
            (both_ref.at[inner_rows, col_blocks], both_ref.at[inner_rows, 0], 1, next_agent),
            (both_ref.at[row_blocks, col_blocks], both_ref.at[0, 0], 2, across),
        ),
        ((rows_ref.at[row_blocks], rows_ref.at[0], 3, next_tile),),
        ((cols_ref.at[col_blocks], cols_ref.at[0], 4, next_agent),),
    )

    def edge_copies(which):
        return [copy(source, target, edge_send, edge_recv, step, to)
                for source, target, step, to in edges[which]]

    for which in nets:

        def add_terms(step):
            term_copy(which)(step).wait_recv()
            terms[which, 0] += term_parts[which, step]

        over(agents, add_terms)
        total = terms[which, 0]
        if which == 0:
            both_ref[1:, 1:] = total.reshape((row_blocks, col_blocks) + both_ref.shape[2:])
        elif which == 1:
            rows_ref[1:] = total.reshape((row_blocks,) + rows_ref.shape[1:])
        else:
            cols_ref[1:] = total.reshape((col_blocks,) + cols_ref.shape[1:])
        for edge in edge_copies(which):
            edge.start()
    for which in nets:
        for edge in edge_copies(which):
            edge.wait()
    over(tiles, lambda step: tile_copy(step).wait_send())
    for which in nets:
        over(agents, lambda step: patch_copy(which)(step).wait_send())
        over(agents, lambda step: term_copy(which)(step).wait_send())
    over(agents, lambda step: sum_copy(step).wait_send())
    over(agents, lambda step: own_copy(step).wait_send())
    over(tiles, lambda step: every_copy(step).wait_send())


def exchange(
    factor, window, starts, volume, lows, fracs, target, patches, up_weight, down_weight, blocks
):
    tiles, agents = lax.axis_size("tile"), lax.axis_size("agent")
    planes, own = target.shape
    row_blocks, col_blocks = blocks
    bins = tiles * agents * own // lows.shape[0]
    whole = pl.BlockSpec(memory_space=pltpu.VMEM)
    count, pixels = patches.shape[1:]
    shapes = (
        (row_blocks + 1, col_blocks + 1, count // (row_blocks * col_blocks), pixels),
        (row_blocks + 1, count // row_blocks, pixels),
        (col_blocks + 1, count // col_blocks, pixels),
    )
    parts = tuple(jax.ShapeDtypeStruct(shape, jnp.float32) for shape in shapes)
    sems = [pltpu.SemaphoreType.DMA((n,)) for n in (
        tiles, tiles, agents, agents, agents, agents, tiles, tiles)]
    sems += [pltpu.SemaphoreType.DMA((patches.shape[0], agents))] * 4
    sems += [pltpu.SemaphoreType.DMA((5,))] * 2
    by_net = (patches.shape[0], agents) + patches.shape[1:]
    return pl.pallas_call(
        functools.partial(exchange_kernel, factor, window, bins, agents),
        out_shape=(jax.ShapeDtypeStruct(volume.shape, jnp.float32),) + parts,
        in_specs=[pl.BlockSpec(memory_space=pltpu.SMEM)] + [whole] * 7,
        out_specs=(whole,) * 4,
        scratch_shapes=[
            pltpu.VMEM((tiles * agents, planes, own), jnp.float32),
            pltpu.VMEM((tiles, agents, planes, own), jnp.float32),
            pltpu.VMEM((agents, planes, own), jnp.float32),
            pltpu.VMEM((agents, planes, own), jnp.float32),
            pltpu.VMEM((tiles * agents, planes, own), jnp.float32),
            pltpu.VMEM(by_net, jnp.bfloat16),
            pltpu.VMEM(by_net, jnp.float32),
            pltpu.VMEM(by_net, jnp.float32),
            *sems,
        ],
        compiler_params=pltpu.CompilerParams(
            collective_id=0, has_side_effects=True, vmem_limit_bytes=48 * 2**20
        ),
        name="exchange",
    )(starts, volume, lows, fracs, target, patches, up_weight, down_weight)


def permute(block, step_tile, step_agent):
    tiles, agents = lax.axis_size("tile"), lax.axis_size("agent")
    pairs = []
    for tile in range(tiles):
        for agent in range(agents):
            source = (tile + step_tile) % tiles * agents + (agent + step_agent) % agents
            pairs.append((source, tile * agents + agent))
    return lax.ppermute(block, ("tile", "agent"), pairs)


def pad_lanes(block):
    short = -block.shape[-1] % LANES
    return jnp.pad(block, ((0, 0),) * (block.ndim - 1) + ((0, short),))


def ahead_kernel(offsets_ref, both_ref, rows_ref, cols_ref, out_ref):
    planes, rows, cols = out_ref.shape[1:]

    def ahead(block, shift, axis):
        return pltpu.roll(block, block.shape[axis] - shift, axis)

    first = ahead(both_ref[...], offsets_ref[0], 1)[:, :rows]
    first = ahead(first, offsets_ref[0], 2)
    second = ahead(rows_ref[...], offsets_ref[1], 1)
    third = ahead(cols_ref[...], offsets_ref[2], 2)
    out_ref[0] = first[:, :, :cols].astype(out_ref.dtype)
    out_ref[1] = second[:, :rows, :cols].astype(out_ref.dtype)
    out_ref[2] = third[:, :, :cols].astype(out_ref.dtype)


def make_patches(noisy, offsets):
    times, slices, rows, cols = noisy.shape[1:]
    row_blocks, col_blocks = rows // PATCH, cols // PATCH
    flat = noisy.reshape(3, times * slices, rows, cols)
    below = permute(flat[:2, :, :PATCH], 1, 0)
    sides = jnp.stack([flat[0, :, :, :PATCH], flat[2, :, :, :PATCH]])
    beyond = permute(sides, 0, 1)
    corner = permute(flat[0, :, :PATCH, :PATCH], 1, 1)
    top = jnp.concatenate([flat[0], beyond[0]], axis=2)
    bottom = jnp.concatenate([below[0], corner], axis=2)
    both = pad_lanes(jnp.concatenate([top, bottom], axis=1).astype(jnp.float32))
    tall = pad_lanes(jnp.concatenate([flat[1], below[1]], axis=1).astype(jnp.float32))
    broad = pad_lanes(jnp.concatenate([flat[2], beyond[1]], axis=2).astype(jnp.float32))
    vmem = pl.BlockSpec(memory_space=pltpu.VMEM)
    moved = pl.pallas_call(
        ahead_kernel,
        out_shape=jax.ShapeDtypeStruct(flat.shape, jnp.float32),
        in_specs=[pl.BlockSpec(memory_space=pltpu.SMEM), vmem, vmem, vmem],
        out_specs=vmem,
        compiler_params=pltpu.CompilerParams(vmem_limit_bytes=32 * 2**20),
        name="ahead",
    )(offsets, both, tall, broad)
    first = moved[0].reshape(times * slices, row_blocks, PATCH, col_blocks, PATCH)
    first = first.transpose(1, 3, 0, 2, 4).reshape(-1, PATCH * PATCH)
    second = moved[1].reshape(times, slices, row_blocks, PATCH, cols)
    second = second.transpose(2, 0, 4, 1, 3).reshape(-1, slices * PATCH)
    third = moved[2].reshape(times, slices, rows, col_blocks, PATCH)
    third = third.transpose(3, 0, 2, 1, 4).reshape(-1, slices * PATCH)
    return jnp.stack([first, second, third]).astype(jnp.bfloat16)


def join_kernel(offsets_ref, weights_ref, state_ref, fit_ref, both_ref, rows_ref, cols_ref, out_ref):
    planes, rows, cols = fit_ref.shape

    def back(block, shift, axis):
        return pltpu.roll(block, block.shape[axis] - (PATCH - shift), axis)

    first = back(both_ref[...], offsets_ref[0], 1)[:, :rows]
    first = back(first, offsets_ref[0], 2)[:, :, :cols]
    second = back(rows_ref[...], offsets_ref[1], 1)[:, :rows, :cols]
    third = back(cols_ref[...], offsets_ref[2], 2)[:, :, :cols]
    answers = [fit_ref[...]]
    for which, removed in enumerate((first, second, third)):
        answers.append(state_ref[which + 1] - removed)
    total = weights_ref[0]
    for which in range(1, len(answers)):
        total = total + weights_ref[which]
    joined = jnp.zeros_like(answers[0])
    for which, answer in enumerate(answers):
        share = jnp.full(joined.shape, weights_ref[which]) / jnp.full(joined.shape, total)
        joined = joined + share * (2.0 * answer - state_ref[which])
    for which, answer in enumerate(answers):
        out_ref[which] = state_ref[which] + joined - answer


def spread_nets(nets, shape):
    times, slices, rows, cols = shape
    planes = times * slices
    tall_blocks, broad_blocks = rows // PATCH + 1, cols // PATCH + 1

    def in_columns(block):
        block = block.reshape(tall_blocks, -1, planes, PATCH, PATCH)
        return block.transpose(2, 0, 3, 1, 4).reshape(planes, rows + PATCH, -1)

    both = jnp.concatenate([in_columns(nets[0][:, :1]), in_columns(nets[0][:, 1:])], axis=2)
    tall = nets[1].reshape(tall_blocks, times, cols, slices, PATCH)
    tall = tall.transpose(1, 3, 0, 4, 2).reshape(planes, rows + PATCH, cols)
    broad = nets[2].reshape(broad_blocks, times, rows, slices, PATCH)
    broad = broad.transpose(1, 3, 2, 0, 4).reshape(planes, rows, cols + PATCH)
    return pad_lanes(both), pad_lanes(tall), pad_lanes(broad)


def join(offsets, weights, state, data_fit, both, tall, broad):
    agents, times, slices, rows, cols = state.shape
    vmem = pl.BlockSpec(memory_space=pltpu.VMEM)
    smem = pl.BlockSpec(memory_space=pltpu.SMEM)
    flat = state.reshape(agents, times * slices, rows, cols)
    out = pl.pallas_call(
        join_kernel,
        out_shape=jax.ShapeDtypeStruct(flat.shape, jnp.float32),
        in_specs=[smem, smem, vmem, vmem, vmem, vmem, vmem],
        out_specs=vmem,
        compiler_params=pltpu.CompilerParams(vmem_limit_bytes=32 * 2**20),
        name="join",
    )(offsets, weights, flat, data_fit.reshape(flat.shape[1:]), both, tall, broad)
    return out.reshape(state.shape)


def data_and_nets(
    volume, bin_index, bin_frac, measured, factor, patches, up_weight, down_weight
):
    angles = bin_index.shape[0]
    planes = volume.shape[0] * volume.shape[1]
    current = volume.reshape(planes, -1)
    tiles, agents, own = lax.axis_size("tile"), lax.axis_size("agent"), measured.shape[2]
    bins = tiles * agents * own // angles
    window = -(-(bin_index.shape[1] + bin_index.shape[2] + 2) // LANES) * LANES
    window = min(window, bins)
    lows = bin_index.reshape(angles, -1)
    fracs = bin_frac.reshape(angles, -1)
    corners = bin_index[:, :: bin_index.shape[1] - 1, :: bin_index.shape[2] - 1]
    starts = jnp.minimum(jnp.min(corners, axis=(1, 2)), bins - window)
    result, *nets = exchange(
        factor, window, starts, current, lows, fracs, measured.reshape(planes, own), patches,
        up_weight, down_weight, (bin_index.shape[1] // PATCH, bin_index.shape[2] // PATCH),
    )
    return result.reshape(volume.shape), nets


def shards(
    agent_state, measured, bin_index, bin_frac, patch_offsets, agent_weights, up_weight, down_weight
):
    row_count = agent_state.shape[3]
    col_count = agent_state.shape[4]
    tile_count = lax.axis_size("tile")
    agent_count = lax.axis_size("agent")
    full_rows = row_count * tile_count
    full_cols = col_count * agent_count
    angles = bin_index.shape[0]
    factor = 1.0 / math.sqrt(angles * (full_rows + full_cols))
    patches = make_patches(agent_state[1:].astype(jnp.bfloat16), patch_offsets)
    data_fit, nets = data_and_nets(
        agent_state[0], bin_index, bin_frac, measured, factor, patches, up_weight, down_weight
    )
    parts = spread_nets(nets, agent_state.shape[1:])
    state_next = join(patch_offsets, agent_weights, agent_state, data_fit, *parts)
    return (state_next, data_fit)


def solution(mesh):
    placed = (
        P(None, None, None, "tile", "agent"),
        P(None, None, ("tile", "agent")),
        P(None, "tile", "agent"),
        P(None, "tile", "agent"),
        P(),
        P(),
        P(None, None, "agent"),
        P(None, "agent", None),
    )
    return jax.shard_map(
        shards,
        mesh=mesh,
        in_specs=placed,
        out_specs=(P(None, None, None, "tile", "agent"), P(None, None, "tile", "agent")),
        check_vma=False,
    )
```

```python
import functools
import math

import jax
import jax.numpy as jnp
from jax import lax
from jax.experimental import pallas as pl
from jax.experimental.pallas import tpu as pltpu
from jax.sharding import PartitionSpec as P

PATCH = 16
LANES = 128
DENOM = 724.0


def split_pair(values):
    high = values.astype(jnp.bfloat16)
    low = (values - high.astype(jnp.float32)).astype(jnp.bfloat16)
    return high, low


def interpolation_rows(low_ref, frac_ref, angle, start, window):
    lows = low_ref[pl.ds(angle, 1), :] - start
    near = frac_ref[pl.ds(angle, 1), :].astype(jnp.float32) / DENOM
    far = 1.0 - near
    near_high = near.astype(jnp.bfloat16).astype(jnp.float32)
    far_high = far.astype(jnp.bfloat16).astype(jnp.float32)
    near_low, far_low = near - near_high, far - far_high
    apart = lax.broadcasted_iota(jnp.int32, (window, lows.shape[1]), 0) - lows
    at_near, at_far = apart == 0, apart == 1
    high = jnp.where(at_near, near_high, jnp.where(at_far, far_high, 0.0))
    low = jnp.where(at_near, near_low, jnp.where(at_far, far_low, 0.0))
    return jnp.concatenate([high.astype(jnp.bfloat16), low.astype(jnp.bfloat16)], axis=0)


def project(factor, window, bins, starts_ref, volume_ref, low_ref, frac_ref, sino_ref):
    angles, (planes, own) = low_ref.shape[0], sino_ref.shape[1:]
    parts = bins // own
    high, low = split_pair(volume_ref[...])
    stacked = jnp.concatenate([high, low], axis=0)

    def step(angle, carry):
        start = starts_ref[angle]
        rows = interpolation_rows(low_ref, frac_ref, angle, start, window)
        out = lax.dot_general(
            stacked, rows, (((1,), (1,)), ((), ())), preferred_element_type=jnp.float32
        )
        out = out[:planes] + out[planes:]
        out = factor * (out[:, :window] + out[:, window:])
        if bins > window:
            out = jnp.concatenate([out, jnp.zeros((planes, bins - window), jnp.float32)], axis=1)
            out = pltpu.roll(out, start, 1)
        for part in range(parts):
            sino_ref[angle * parts + part] = out[:, part * own : (part + 1) * own]
        return carry

    lax.fori_loop(0, angles, step, 0, unroll=4)


def spread(factor, window, bins, starts_ref, misfit_ref, low_ref, frac_ref, volume_ref, out_ref):
    angles, (planes, own) = low_ref.shape[0], misfit_ref.shape[1:]
    parts = bins // own
    out_ref[...] = volume_ref[...]

    def step(angle, carry):
        start = starts_ref[angle]
        rows = interpolation_rows(low_ref, frac_ref, angle, start, window)
        resid = jnp.concatenate(
            [misfit_ref[angle * parts + part] for part in range(parts)], axis=1
        )
        if bins > window:
            resid = pltpu.roll(resid, bins - start, 1)[:, :window]
        high, low = split_pair(resid)
        left = jnp.concatenate([high, low], axis=0)
        left = jnp.concatenate([left, left], axis=1)
        out = jnp.dot(left, rows, preferred_element_type=jnp.float32)
        out_ref[...] -= factor * (out[:planes] + out[planes:])
        return carry

    lax.fori_loop(0, angles, step, 0, unroll=4)


def exchange_kernel(
    factor, window, bins, agents,
    starts_ref, volume_ref, low_ref, frac_ref, target_ref, patches_ref, up_ref, down_ref,
    fit_ref, both_ref, rows_ref, cols_ref,
    chunks, tile_parts, band, agent_parts, every, wide, terms, term_parts,
    tile_send, tile_recv, sum_send, sum_recv, own_send, own_recv,
    every_send, every_recv, patch_send, patch_recv, term_send, term_recv,
    edge_send, edge_recv,
):
    tiles = chunks.shape[0] // agents
    tile, agent = lax.axis_index("tile"), lax.axis_index("agent")
    mine = tile * agents + agent

    def tile_at(step):
        return lax.rem(tile + step, tiles)

    def agent_at(step):
        return lax.rem(agent + step, agents)

    def copy(source, target, send, recv, step, to):
        return pltpu.make_async_remote_copy(
            src_ref=source,
            dst_ref=target,
            send_sem=send.at[step],
            recv_sem=recv.at[step],
            device_id=to,
            device_id_type=pl.DeviceIdType.MESH,
        )

    def share_of(which):
        return pl.ds(which * agents, agents)

    def to_tile(step):
        return (tile_at(step), agent)

    def to_agent(step):
        return (tile, agent_at(step))

    def over(count, body):
        def step_body(step, carry):
            body(step)
            return carry

        lax.fori_loop(1, count, step_body, 0)

    barrier = pltpu.get_barrier_semaphore()
    over(agents, lambda step: pl.semaphore_signal(
        barrier, inc=1, device_id=to_agent(step), device_id_type=pl.DeviceIdType.MESH))
    over(tiles, lambda step: pl.semaphore_signal(
        barrier, inc=1, device_id=to_tile(step), device_id_type=pl.DeviceIdType.MESH))
    pl.semaphore_signal(
        barrier, inc=1, device_id=(tile_at(tiles - 1), agent_at(agents - 1)),
        device_id_type=pl.DeviceIdType.MESH)
    pl.semaphore_wait(barrier, tiles + agents - 1)

    def tile_copy(step):
        return copy(
            chunks.at[share_of(tile_at(step))], tile_parts.at[step], tile_send, tile_recv, step,
            to_tile(step))

    def patch_copy(which):
        return lambda step: copy(
            patches_ref.at[which], wide.at[which, step], patch_send.at[which],
            patch_recv.at[which], step, to_agent(step))

    def sum_copy(step):
        return copy(
            band.at[agent_at(step)], agent_parts.at[step], sum_send, sum_recv, step,
            to_agent(step))

    def own_copy(step):
        return copy(
            every.at[mine], every.at[mine], own_send, own_recv, step,
            to_agent(step))

    def own_arrival(step):
        where = every.at[tile * agents + agent_at(agents - step)]
        return copy(where, where, own_send, own_recv, step, to_agent(step))

    def every_copy(step):
        return copy(
            every.at[share_of(tile)], every.at[share_of(tile)], every_send, every_recv, step, to_tile(step))

    def every_arrival(step):
        where = every.at[share_of(tile_at(tiles - step))]
        return copy(where, where, every_send, every_recv, step, to_tile(step))

    def term_copy(which):
        return lambda step: copy(
            terms.at[which, agents - step], term_parts.at[which, step], term_send.at[which],
            term_recv.at[which], step, to_agent(step))

    nets = range(patches_ref.shape[0])
    count = patches_ref.shape[1]

    def run_net(which):
        over(agents, lambda step: patch_copy(which)(step).wait_recv())
        rows = wide[which].reshape(agents * count, patches_ref.shape[2])
        hidden = jnp.dot(rows, up_ref[which], preferred_element_type=jnp.float32)
        hidden = jnp.maximum(hidden, 0.0).astype(jnp.bfloat16)
        out = jnp.dot(hidden, down_ref[which], preferred_element_type=jnp.float32)
        terms[which] = out.reshape(agents, count, out.shape[1])

    def add_tile(step):
        tile_copy(step).wait_recv()
        band[...] += tile_parts[step]

    def add_agent(step):
        sum_copy(step).wait_recv()
        every[mine] += agent_parts[step]

    for which in nets:
        over(agents, lambda step: patch_copy(which)(step).start())
        wide[which, 0] = patches_ref[which]
    project(factor, window, bins, starts_ref, volume_ref, low_ref, frac_ref, chunks)
    over(tiles, lambda step: tile_copy(step).start())
    band[...] = chunks[share_of(tile)]
    run_net(0)
    run_net(1)
    over(tiles, add_tile)
    over(agents, lambda step: sum_copy(step).start())
    every[mine] = band[agent] - target_ref[...]
    run_net(2)
    over(agents, add_agent)
    over(agents, lambda step: own_copy(step).start())
    for which in nets:
        over(agents, lambda step: term_copy(which)(step).start())
    over(agents, lambda step: own_arrival(step).wait_recv())
    over(tiles, lambda step: every_copy(step).start())
    over(tiles, lambda step: every_arrival(step).wait_recv())
    spread(factor, window, bins, starts_ref, every, low_ref, frac_ref, volume_ref, fit_ref)
    row_blocks, col_blocks = both_ref.shape[0] - 1, both_ref.shape[1] - 1
    next_tile, next_agent = to_tile(1), to_agent(1)
    across = (next_tile[0], next_agent[1])
    inner_rows, inner_cols = pl.ds(1, row_blocks), pl.ds(1, col_blocks)
    edges = (
        (
            (both_ref.at[row_blocks, inner_cols], both_ref.at[0, inner_cols], 0, next_tile),
            (both_ref.at[inner_rows, col_blocks], both_ref.at[inner_rows, 0], 1, next_agent),
            (both_ref.at[row_blocks, col_blocks], both_ref.at[0, 0], 2, across),
        ),
        ((rows_ref.at[row_blocks], rows_ref.at[0], 3, next_tile),),
        ((cols_ref.at[col_blocks], cols_ref.at[0], 4, next_agent),),
    )

    def edge_copies(which):
        return [copy(source, target, edge_send, edge_recv, step, to)
                for source, target, step, to in edges[which]]

    for which in nets:

        def add_terms(step):
            term_copy(which)(step).wait_recv()
            terms[which, 0] += term_parts[which, step]

        over(agents, add_terms)
        total = terms[which, 0]
        if which == 0:
            both_ref[1:, 1:] = total.reshape((row_blocks, col_blocks) + both_ref.shape[2:])
        elif which == 1:
            rows_ref[1:] = total.reshape((row_blocks,) + rows_ref.shape[1:])
        else:
            cols_ref[1:] = total.reshape((col_blocks,) + cols_ref.shape[1:])
        for edge in edge_copies(which):
            edge.start()
    for which in nets:
        for edge in edge_copies(which):
            edge.wait()
    over(tiles, lambda step: tile_copy(step).wait_send())
    for which in nets:
        over(agents, lambda step: patch_copy(which)(step).wait_send())
        over(agents, lambda step: term_copy(which)(step).wait_send())
    over(agents, lambda step: sum_copy(step).wait_send())
    over(agents, lambda step: own_copy(step).wait_send())
    over(tiles, lambda step: every_copy(step).wait_send())


def exchange(
    factor, window, starts, volume, lows, fracs, target, patches, up_weight, down_weight, blocks
):
    tiles, agents = lax.axis_size("tile"), lax.axis_size("agent")
    planes, own = target.shape
    row_blocks, col_blocks = blocks
    bins = tiles * agents * own // lows.shape[0]
    whole = pl.BlockSpec(memory_space=pltpu.VMEM)
    count, pixels = patches.shape[1:]
    shapes = (
        (row_blocks + 1, col_blocks + 1, count // (row_blocks * col_blocks), pixels),
        (row_blocks + 1, count // row_blocks, pixels),
        (col_blocks + 1, count // col_blocks, pixels),
    )
    parts = tuple(jax.ShapeDtypeStruct(shape, jnp.float32) for shape in shapes)
    sems = [pltpu.SemaphoreType.DMA((n,)) for n in (
        tiles, tiles, agents, agents, agents, agents, tiles, tiles)]
    sems += [pltpu.SemaphoreType.DMA((patches.shape[0], agents))] * 4
    sems += [pltpu.SemaphoreType.DMA((5,))] * 2
    by_net = (patches.shape[0], agents) + patches.shape[1:]
    return pl.pallas_call(
        functools.partial(exchange_kernel, factor, window, bins, agents),
        out_shape=(jax.ShapeDtypeStruct(volume.shape, jnp.float32),) + parts,
        in_specs=[pl.BlockSpec(memory_space=pltpu.SMEM)] + [whole] * 7,
        out_specs=(whole,) * 4,
        scratch_shapes=[
            pltpu.VMEM((tiles * agents, planes, own), jnp.float32),
            pltpu.VMEM((tiles, agents, planes, own), jnp.float32),
            pltpu.VMEM((agents, planes, own), jnp.float32),
            pltpu.VMEM((agents, planes, own), jnp.float32),
            pltpu.VMEM((tiles * agents, planes, own), jnp.float32),
            pltpu.VMEM(by_net, jnp.bfloat16),
            pltpu.VMEM(by_net, jnp.float32),
            pltpu.VMEM(by_net, jnp.float32),
            *sems,
        ],
        compiler_params=pltpu.CompilerParams(
            collective_id=0, has_side_effects=True, vmem_limit_bytes=48 * 2**20
        ),
        name="exchange",
    )(starts, volume, lows, fracs, target, patches, up_weight, down_weight)


def permute(block, step_tile, step_agent):
    tiles, agents = lax.axis_size("tile"), lax.axis_size("agent")
    pairs = []
    for tile in range(tiles):
        for agent in range(agents):
            source = (tile + step_tile) % tiles * agents + (agent + step_agent) % agents
            pairs.append((source, tile * agents + agent))
    return lax.ppermute(block, ("tile", "agent"), pairs)


def pad_lanes(block):
    short = -block.shape[-1] % LANES
    return jnp.pad(block, ((0, 0),) * (block.ndim - 1) + ((0, short),))


def ahead_kernel(offsets_ref, both_ref, rows_ref, cols_ref, out_ref):
    planes, rows, cols = out_ref.shape[1:]

    def ahead(block, shift, axis):
        return pltpu.roll(block, block.shape[axis] - shift, axis)

    first = ahead(both_ref[...], offsets_ref[0], 1)[:, :rows]
    first = ahead(first, offsets_ref[0], 2)
    second = ahead(rows_ref[...], offsets_ref[1], 1)
    third = ahead(cols_ref[...], offsets_ref[2], 2)
    out_ref[0] = first[:, :, :cols].astype(out_ref.dtype)
    out_ref[1] = second[:, :rows, :cols].astype(out_ref.dtype)
    out_ref[2] = third[:, :, :cols].astype(out_ref.dtype)


def make_patches(noisy, offsets):
    times, slices, rows, cols = noisy.shape[1:]
    row_blocks, col_blocks = rows // PATCH, cols // PATCH
    flat = noisy.reshape(3, times * slices, rows, cols)
    below = permute(flat[:2, :, :PATCH], 1, 0)
    sides = jnp.stack([flat[0, :, :, :PATCH], flat[2, :, :, :PATCH]])
    beyond = permute(sides, 0, 1)
    corner = permute(flat[0, :, :PATCH, :PATCH], 1, 1)
    top = jnp.concatenate([flat[0], beyond[0]], axis=2)
    bottom = jnp.concatenate([below[0], corner], axis=2)
    both = pad_lanes(jnp.concatenate([top, bottom], axis=1).astype(jnp.float32))
    tall = pad_lanes(jnp.concatenate([flat[1], below[1]], axis=1).astype(jnp.float32))
    broad = pad_lanes(jnp.concatenate([flat[2], beyond[1]], axis=2).astype(jnp.float32))
    vmem = pl.BlockSpec(memory_space=pltpu.VMEM)
    moved = pl.pallas_call(
        ahead_kernel,
        out_shape=jax.ShapeDtypeStruct(flat.shape, jnp.float32),
        in_specs=[pl.BlockSpec(memory_space=pltpu.SMEM), vmem, vmem, vmem],
        out_specs=vmem,
        compiler_params=pltpu.CompilerParams(vmem_limit_bytes=32 * 2**20),
        name="ahead",
    )(offsets, both, tall, broad)
    first = moved[0].reshape(times * slices, row_blocks, PATCH, col_blocks, PATCH)
    first = first.transpose(1, 3, 0, 2, 4).reshape(-1, PATCH * PATCH)
    second = moved[1].reshape(times, slices, row_blocks, PATCH, cols)
    second = second.transpose(2, 0, 4, 1, 3).reshape(-1, slices * PATCH)
    third = moved[2].reshape(times, slices, rows, col_blocks, PATCH)
    third = third.transpose(3, 0, 2, 1, 4).reshape(-1, slices * PATCH)
    return jnp.stack([first, second, third]).astype(jnp.bfloat16)


def join_kernel(offsets_ref, weights_ref, state_ref, fit_ref, both_ref, rows_ref, cols_ref, out_ref):
    planes, rows, cols = fit_ref.shape

    def back(block, shift, axis):
        return pltpu.roll(block, block.shape[axis] - (PATCH - shift), axis)

    first = back(both_ref[...], offsets_ref[0], 1)[:, :rows]
    first = back(first, offsets_ref[0], 2)[:, :, :cols]
    second = back(rows_ref[...], offsets_ref[1], 1)[:, :rows, :cols]
    third = back(cols_ref[...], offsets_ref[2], 2)[:, :, :cols]
    answers = [fit_ref[...]]
    for which, removed in enumerate((first, second, third)):
        answers.append(state_ref[which + 1] - removed)
    total = weights_ref[0]
    for which in range(1, len(answers)):
        total = total + weights_ref[which]
    joined = jnp.zeros_like(answers[0])
    for which, answer in enumerate(answers):
        share = jnp.full(joined.shape, weights_ref[which]) / jnp.full(joined.shape, total)
        joined = joined + share * (2.0 * answer - state_ref[which])
    for which, answer in enumerate(answers):
        out_ref[which] = state_ref[which] + joined - answer


def spread_nets(nets, shape):
    times, slices, rows, cols = shape
    planes = times * slices
    tall_blocks, broad_blocks = rows // PATCH + 1, cols // PATCH + 1

    def in_columns(block):
        block = block.reshape(tall_blocks, -1, planes, PATCH, PATCH)
        return block.transpose(2, 0, 3, 1, 4).reshape(planes, rows + PATCH, -1)

    both = jnp.concatenate([in_columns(nets[0][:, :1]), in_columns(nets[0][:, 1:])], axis=2)
    tall = nets[1].reshape(tall_blocks, times, cols, slices, PATCH)
    tall = tall.transpose(1, 3, 0, 4, 2).reshape(planes, rows + PATCH, cols)
    broad = nets[2].reshape(broad_blocks, times, rows, slices, PATCH)
    broad = broad.transpose(1, 3, 2, 0, 4).reshape(planes, rows, cols + PATCH)
    return pad_lanes(both), pad_lanes(tall), pad_lanes(broad)


def join(offsets, weights, state, data_fit, both, tall, broad):
    agents, times, slices, rows, cols = state.shape
    vmem = pl.BlockSpec(memory_space=pltpu.VMEM)
    smem = pl.BlockSpec(memory_space=pltpu.SMEM)
    flat = state.reshape(agents, times * slices, rows, cols)
    out = pl.pallas_call(
        join_kernel,
        out_shape=jax.ShapeDtypeStruct(flat.shape, jnp.float32),
        in_specs=[smem, smem, vmem, vmem, vmem, vmem, vmem],
        out_specs=vmem,
        compiler_params=pltpu.CompilerParams(vmem_limit_bytes=32 * 2**20),
        name="join",
    )(offsets, weights, flat, data_fit.reshape(flat.shape[1:]), both, tall, broad)
    return out.reshape(state.shape)


def data_and_nets(
    volume, bin_index, bin_frac, measured, factor, patches, up_weight, down_weight
):
    angles = bin_index.shape[0]
    planes = volume.shape[0] * volume.shape[1]
    current = volume.reshape(planes, -1)
    tiles, agents, own = lax.axis_size("tile"), lax.axis_size("agent"), measured.shape[2]
    bins = tiles * agents * own // angles
    window = -(-(bin_index.shape[1] + bin_index.shape[2] + 2) // LANES) * LANES
    window = min(window, bins)
    lows = bin_index.reshape(angles, -1)
    fracs = bin_frac.reshape(angles, -1)
    corners = bin_index[:, :: bin_index.shape[1] - 1, :: bin_index.shape[2] - 1]
    starts = jnp.minimum(jnp.min(corners, axis=(1, 2)), bins - window)
    result, *nets = exchange(
        factor, window, starts, current, lows, fracs, measured.reshape(planes, own), patches,
        up_weight, down_weight, (bin_index.shape[1] // PATCH, bin_index.shape[2] // PATCH),
    )
    return result.reshape(volume.shape), nets


def shards(
    agent_state, measured, bin_index, bin_frac, patch_offsets, agent_weights, up_weight, down_weight
):
    row_count = agent_state.shape[3]
    col_count = agent_state.shape[4]
    tile_count = lax.axis_size("tile")
    agent_count = lax.axis_size("agent")
    full_rows = row_count * tile_count
    full_cols = col_count * agent_count
    angles = bin_index.shape[0]
    factor = 1.0 / math.sqrt(angles * (full_rows + full_cols))
    patches = make_patches(agent_state[1:].astype(jnp.bfloat16), patch_offsets)
    data_fit, nets = data_and_nets(
        agent_state[0], bin_index, bin_frac, measured, factor, patches, up_weight, down_weight
    )
    parts = spread_nets(nets, agent_state.shape[1:])
    state_next = join(patch_offsets, agent_weights, agent_state, data_fit, *parts)
    return (state_next, data_fit)


def solution(mesh):
    placed = (
        P(None, None, None, "tile", "agent"),
        P(None, None, ("tile", "agent")),
        P(None, "tile", "agent"),
        P(None, "tile", "agent"),
        P(),
        P(),
        P(None, None, "agent"),
        P(None, "agent", None),
    )
    return jax.shard_map(
        shards,
        mesh=mesh,
        in_specs=placed,
        out_specs=(P(None, None, None, "tile", "agent"), P(None, None, "tile", "agent")),
        check_vma=False,
    )
```

```python
import functools
import math

import jax
import jax.numpy as jnp
from jax import lax
from jax.experimental import pallas as pl
from jax.experimental.pallas import tpu as pltpu
from jax.sharding import PartitionSpec as P

PATCH = 16
LANES = 128
DENOM = 724.0


def split_pair(values):
    high = values.astype(jnp.bfloat16)
    low = (values - high.astype(jnp.float32)).astype(jnp.bfloat16)
    return high, low


def interpolation_rows(low_ref, frac_ref, angle, start, window):
    lows = low_ref[pl.ds(angle, 1), :] - start
    near = frac_ref[pl.ds(angle, 1), :].astype(jnp.float32) / DENOM
    far = 1.0 - near
    near_high = near.astype(jnp.bfloat16).astype(jnp.float32)
    far_high = far.astype(jnp.bfloat16).astype(jnp.float32)
    near_low, far_low = near - near_high, far - far_high
    apart = lax.broadcasted_iota(jnp.int32, (window, lows.shape[1]), 0) - lows
    at_near, at_far = apart == 0, apart == 1
    high = jnp.where(at_near, near_high, jnp.where(at_far, far_high, 0.0))
    low = jnp.where(at_near, near_low, jnp.where(at_far, far_low, 0.0))
    return jnp.concatenate([high.astype(jnp.bfloat16), low.astype(jnp.bfloat16)], axis=0)


def project(factor, window, bins, starts_ref, volume_ref, low_ref, frac_ref, sino_ref):
    angles, (planes, own) = low_ref.shape[0], sino_ref.shape[1:]
    parts = bins // own
    high, low = split_pair(volume_ref[...])
    stacked = jnp.concatenate([high, low], axis=0)

    def step(angle, carry):
        start = starts_ref[angle]
        rows = interpolation_rows(low_ref, frac_ref, angle, start, window)
        out = lax.dot_general(
            stacked, rows, (((1,), (1,)), ((), ())), preferred_element_type=jnp.float32
        )
        out = out[:planes] + out[planes:]
        out = factor * (out[:, :window] + out[:, window:])
        if bins > window:
            out = jnp.concatenate([out, jnp.zeros((planes, bins - window), jnp.float32)], axis=1)
            out = pltpu.roll(out, start, 1)
        for part in range(parts):
            sino_ref[angle * parts + part] = out[:, part * own : (part + 1) * own]
        return carry

    lax.fori_loop(0, angles, step, 0, unroll=4)


def spread(factor, window, bins, starts_ref, misfit_ref, low_ref, frac_ref, volume_ref, out_ref):
    angles, (planes, own) = low_ref.shape[0], misfit_ref.shape[1:]
    parts = bins // own
    out_ref[...] = volume_ref[...]

    def step(angle, carry):
        start = starts_ref[angle]
        rows = interpolation_rows(low_ref, frac_ref, angle, start, window)
        resid = jnp.concatenate(
            [misfit_ref[angle * parts + part] for part in range(parts)], axis=1
        )
        if bins > window:
            resid = pltpu.roll(resid, bins - start, 1)[:, :window]
        high, low = split_pair(resid)
        left = jnp.concatenate([high, low], axis=0)
        left = jnp.concatenate([left, left], axis=1)
        out = jnp.dot(left, rows, preferred_element_type=jnp.float32)
        out_ref[...] -= factor * (out[:planes] + out[planes:])
        return carry

    lax.fori_loop(0, angles, step, 0, unroll=4)


def exchange_kernel(
    factor, window, bins, agents,
    starts_ref, volume_ref, low_ref, frac_ref, target_ref, patches_ref, up_ref, down_ref,
    fit_ref, both_ref, rows_ref, cols_ref,
    chunks, tile_parts, band, agent_parts, every, wide, terms, term_parts,
    tile_send, tile_recv, sum_send, sum_recv, own_send, own_recv,
    every_send, every_recv, patch_send, patch_recv, term_send, term_recv,
    edge_send, edge_recv,
):
    tiles = chunks.shape[0] // agents
    tile, agent = lax.axis_index("tile"), lax.axis_index("agent")
    mine = tile * agents + agent

    def tile_at(step):
        return lax.rem(tile + step, tiles)

    def agent_at(step):
        return lax.rem(agent + step, agents)

    def copy(source, target, send, recv, step, to):
        return pltpu.make_async_remote_copy(
            src_ref=source,
            dst_ref=target,
            send_sem=send.at[step],
            recv_sem=recv.at[step],
            device_id=to,
            device_id_type=pl.DeviceIdType.MESH,
        )

    def share_of(which):
        return pl.ds(which * agents, agents)

    def to_tile(step):
        return (tile_at(step), agent)

    def to_agent(step):
        return (tile, agent_at(step))

    def over(count, body):
        def step_body(step, carry):
            body(step)
            return carry

        lax.fori_loop(1, count, step_body, 0)

    barrier = pltpu.get_barrier_semaphore()
    over(agents, lambda step: pl.semaphore_signal(
        barrier, inc=1, device_id=to_agent(step), device_id_type=pl.DeviceIdType.MESH))
    over(tiles, lambda step: pl.semaphore_signal(
        barrier, inc=1, device_id=to_tile(step), device_id_type=pl.DeviceIdType.MESH))
    pl.semaphore_signal(
        barrier, inc=1, device_id=(tile_at(tiles - 1), agent_at(agents - 1)),
        device_id_type=pl.DeviceIdType.MESH)
    pl.semaphore_wait(barrier, tiles + agents - 1)

    def tile_copy(step):
        return copy(
            chunks.at[share_of(tile_at(step))], tile_parts.at[step], tile_send, tile_recv, step,
            to_tile(step))

    def patch_copy(which):
        return lambda step: copy(
            patches_ref.at[which], wide.at[which, step], patch_send.at[which],
            patch_recv.at[which], step, to_agent(step))

    def sum_copy(step):
        return copy(
            band.at[agent_at(step)], agent_parts.at[step], sum_send, sum_recv, step,
            to_agent(step))

    def own_copy(step):
        return copy(
            every.at[mine], every.at[mine], own_send, own_recv, step,
            to_agent(step))

    def own_arrival(step):
        where = every.at[tile * agents + agent_at(agents - step)]
        return copy(where, where, own_send, own_recv, step, to_agent(step))

    def every_copy(step):
        return copy(
            every.at[share_of(tile)], every.at[share_of(tile)], every_send, every_recv, step, to_tile(step))

    def every_arrival(step):
        where = every.at[share_of(tile_at(tiles - step))]
        return copy(where, where, every_send, every_recv, step, to_tile(step))

    def term_copy(which):
        return lambda step: copy(
            terms.at[which, agents - step], term_parts.at[which, step], term_send.at[which],
            term_recv.at[which], step, to_agent(step))

    nets = range(patches_ref.shape[0])
    count = patches_ref.shape[1]

    def run_net(which):
        over(agents, lambda step: patch_copy(which)(step).wait_recv())
        rows = wide[which].reshape(agents * count, patches_ref.shape[2])
        hidden = jnp.dot(rows, up_ref[which], preferred_element_type=jnp.float32)
        hidden = jnp.maximum(hidden, 0.0).astype(jnp.bfloat16)
        out = jnp.dot(hidden, down_ref[which], preferred_element_type=jnp.float32)
        terms[which] = out.reshape(agents, count, out.shape[1])

    def add_tile(step):
        tile_copy(step).wait_recv()
        band[...] += tile_parts[step]

    def add_agent(step):
        sum_copy(step).wait_recv()
        every[mine] += agent_parts[step]

    for which in nets:
        over(agents, lambda step: patch_copy(which)(step).start())
        wide[which, 0] = patches_ref[which]
    project(factor, window, bins, starts_ref, volume_ref, low_ref, frac_ref, chunks)
    over(tiles, lambda step: tile_copy(step).start())
    band[...] = chunks[share_of(tile)]
    run_net(0)
    over(agents, lambda step: term_copy(0)(step).start())
    run_net(1)
    over(tiles, add_tile)
    over(agents, lambda step: sum_copy(step).start())
    every[mine] = band[agent] - target_ref[...]
    run_net(2)
    over(agents, add_agent)
    over(agents, lambda step: own_copy(step).start())
    for which in nets[1:]:
        over(agents, lambda step: term_copy(which)(step).start())
    over(agents, lambda step: own_arrival(step).wait_recv())
    over(tiles, lambda step: every_copy(step).start())
    over(tiles, lambda step: every_arrival(step).wait_recv())
    spread(factor, window, bins, starts_ref, every, low_ref, frac_ref, volume_ref, fit_ref)
    row_blocks, col_blocks = both_ref.shape[0] - 1, both_ref.shape[1] - 1
    next_tile, next_agent = to_tile(1), to_agent(1)
    across = (next_tile[0], next_agent[1])
    inner_rows, inner_cols = pl.ds(1, row_blocks), pl.ds(1, col_blocks)
    edges = (
        (
            (both_ref.at[row_blocks, inner_cols], both_ref.at[0, inner_cols], 0, next_tile),
            (both_ref.at[inner_rows, col_blocks], both_ref.at[inner_rows, 0], 1, next_agent),
            (both_ref.at[row_blocks, col_blocks], both_ref.at[0, 0], 2, across),
        ),
        ((rows_ref.at[row_blocks], rows_ref.at[0], 3, next_tile),),
        ((cols_ref.at[col_blocks], cols_ref.at[0], 4, next_agent),),
    )

    def edge_copies(which):
        return [copy(source, target, edge_send, edge_recv, step, to)
                for source, target, step, to in edges[which]]

    for which in nets:

        def add_terms(step):
            term_copy(which)(step).wait_recv()
            terms[which, 0] += term_parts[which, step]

        over(agents, add_terms)
        total = terms[which, 0]
        if which == 0:
            both_ref[1:, 1:] = total.reshape((row_blocks, col_blocks) + both_ref.shape[2:])
        elif which == 1:
            rows_ref[1:] = total.reshape((row_blocks,) + rows_ref.shape[1:])
        else:
            cols_ref[1:] = total.reshape((col_blocks,) + cols_ref.shape[1:])
        for edge in edge_copies(which):
            edge.start()
    for which in nets:
        for edge in edge_copies(which):
            edge.wait()
    over(tiles, lambda step: tile_copy(step).wait_send())
    for which in nets:
        over(agents, lambda step: patch_copy(which)(step).wait_send())
        over(agents, lambda step: term_copy(which)(step).wait_send())
    over(agents, lambda step: sum_copy(step).wait_send())
    over(agents, lambda step: own_copy(step).wait_send())
    over(tiles, lambda step: every_copy(step).wait_send())


def exchange(
    factor, window, starts, volume, lows, fracs, target, patches, up_weight, down_weight, blocks
):
    tiles, agents = lax.axis_size("tile"), lax.axis_size("agent")
    planes, own = target.shape
    row_blocks, col_blocks = blocks
    bins = tiles * agents * own // lows.shape[0]
    whole = pl.BlockSpec(memory_space=pltpu.VMEM)
    count, pixels = patches.shape[1:]
    shapes = (
        (row_blocks + 1, col_blocks + 1, count // (row_blocks * col_blocks), pixels),
        (row_blocks + 1, count // row_blocks, pixels),
        (col_blocks + 1, count // col_blocks, pixels),
    )
    parts = tuple(jax.ShapeDtypeStruct(shape, jnp.float32) for shape in shapes)
    sems = [pltpu.SemaphoreType.DMA((n,)) for n in (
        tiles, tiles, agents, agents, agents, agents, tiles, tiles)]
    sems += [pltpu.SemaphoreType.DMA((patches.shape[0], agents))] * 4
    sems += [pltpu.SemaphoreType.DMA((5,))] * 2
    by_net = (patches.shape[0], agents) + patches.shape[1:]
    return pl.pallas_call(
        functools.partial(exchange_kernel, factor, window, bins, agents),
        out_shape=(jax.ShapeDtypeStruct(volume.shape, jnp.float32),) + parts,
        in_specs=[pl.BlockSpec(memory_space=pltpu.SMEM)] + [whole] * 7,
        out_specs=(whole,) * 4,
        scratch_shapes=[
            pltpu.VMEM((tiles * agents, planes, own), jnp.float32),
            pltpu.VMEM((tiles, agents, planes, own), jnp.float32),
            pltpu.VMEM((agents, planes, own), jnp.float32),
            pltpu.VMEM((agents, planes, own), jnp.float32),
            pltpu.VMEM((tiles * agents, planes, own), jnp.float32),
            pltpu.VMEM(by_net, jnp.bfloat16),
            pltpu.VMEM(by_net, jnp.float32),
            pltpu.VMEM(by_net, jnp.float32),
            *sems,
        ],
        compiler_params=pltpu.CompilerParams(
            collective_id=0, has_side_effects=True, vmem_limit_bytes=48 * 2**20
        ),
        name="exchange",
    )(starts, volume, lows, fracs, target, patches, up_weight, down_weight)


def permute(block, step_tile, step_agent):
    tiles, agents = lax.axis_size("tile"), lax.axis_size("agent")
    pairs = []
    for tile in range(tiles):
        for agent in range(agents):
            source = (tile + step_tile) % tiles * agents + (agent + step_agent) % agents
            pairs.append((source, tile * agents + agent))
    return lax.ppermute(block, ("tile", "agent"), pairs)


def pad_lanes(block):
    short = -block.shape[-1] % LANES
    return jnp.pad(block, ((0, 0),) * (block.ndim - 1) + ((0, short),))


def ahead_kernel(offsets_ref, both_ref, rows_ref, cols_ref, out_ref):
    planes, rows, cols = out_ref.shape[1:]

    def ahead(block, shift, axis):
        return pltpu.roll(block, block.shape[axis] - shift, axis)

    first = ahead(both_ref[...], offsets_ref[0], 1)[:, :rows]
    first = ahead(first, offsets_ref[0], 2)
    second = ahead(rows_ref[...], offsets_ref[1], 1)
    third = ahead(cols_ref[...], offsets_ref[2], 2)
    out_ref[0] = first[:, :, :cols].astype(out_ref.dtype)
    out_ref[1] = second[:, :rows, :cols].astype(out_ref.dtype)
    out_ref[2] = third[:, :, :cols].astype(out_ref.dtype)


def make_patches(noisy, offsets):
    times, slices, rows, cols = noisy.shape[1:]
    row_blocks, col_blocks = rows // PATCH, cols // PATCH
    flat = noisy.reshape(3, times * slices, rows, cols)
    below = permute(flat[:2, :, :PATCH], 1, 0)
    sides = jnp.stack([flat[0, :, :, :PATCH], flat[2, :, :, :PATCH]])
    beyond = permute(sides, 0, 1)
    corner = permute(flat[0, :, :PATCH, :PATCH], 1, 1)
    top = jnp.concatenate([flat[0], beyond[0]], axis=2)
    bottom = jnp.concatenate([below[0], corner], axis=2)
    both = pad_lanes(jnp.concatenate([top, bottom], axis=1).astype(jnp.float32))
    tall = pad_lanes(jnp.concatenate([flat[1], below[1]], axis=1).astype(jnp.float32))
    broad = pad_lanes(jnp.concatenate([flat[2], beyond[1]], axis=2).astype(jnp.float32))
    vmem = pl.BlockSpec(memory_space=pltpu.VMEM)
    moved = pl.pallas_call(
        ahead_kernel,
        out_shape=jax.ShapeDtypeStruct(flat.shape, jnp.float32),
        in_specs=[pl.BlockSpec(memory_space=pltpu.SMEM), vmem, vmem, vmem],
        out_specs=vmem,
        compiler_params=pltpu.CompilerParams(vmem_limit_bytes=32 * 2**20),
        name="ahead",
    )(offsets, both, tall, broad)
    first = moved[0].reshape(times * slices, row_blocks, PATCH, col_blocks, PATCH)
    first = first.transpose(1, 3, 0, 2, 4).reshape(-1, PATCH * PATCH)
    second = moved[1].reshape(times, slices, row_blocks, PATCH, cols)
    second = second.transpose(2, 0, 4, 1, 3).reshape(-1, slices * PATCH)
    third = moved[2].reshape(times, slices, rows, col_blocks, PATCH)
    third = third.transpose(3, 0, 2, 1, 4).reshape(-1, slices * PATCH)
    return jnp.stack([first, second, third]).astype(jnp.bfloat16)


def join_kernel(offsets_ref, weights_ref, state_ref, fit_ref, both_ref, rows_ref, cols_ref, out_ref):
    planes, rows, cols = fit_ref.shape

    def back(block, shift, axis):
        return pltpu.roll(block, block.shape[axis] - (PATCH - shift), axis)

    first = back(both_ref[...], offsets_ref[0], 1)[:, :rows]
    first = back(first, offsets_ref[0], 2)[:, :, :cols]
    second = back(rows_ref[...], offsets_ref[1], 1)[:, :rows, :cols]
    third = back(cols_ref[...], offsets_ref[2], 2)[:, :, :cols]
    answers = [fit_ref[...]]
    for which, removed in enumerate((first, second, third)):
        answers.append(state_ref[which + 1] - removed)
    total = weights_ref[0]
    for which in range(1, len(answers)):
        total = total + weights_ref[which]
    joined = jnp.zeros_like(answers[0])
    for which, answer in enumerate(answers):
        share = jnp.full(joined.shape, weights_ref[which]) / jnp.full(joined.shape, total)
        joined = joined + share * (2.0 * answer - state_ref[which])
    for which, answer in enumerate(answers):
        out_ref[which] = state_ref[which] + joined - answer


def spread_nets(nets, shape):
    times, slices, rows, cols = shape
    planes = times * slices
    tall_blocks, broad_blocks = rows // PATCH + 1, cols // PATCH + 1

    def in_columns(block):
        block = block.reshape(tall_blocks, -1, planes, PATCH, PATCH)
        return block.transpose(2, 0, 3, 1, 4).reshape(planes, rows + PATCH, -1)

    both = jnp.concatenate([in_columns(nets[0][:, :1]), in_columns(nets[0][:, 1:])], axis=2)
    tall = nets[1].reshape(tall_blocks, times, cols, slices, PATCH)
    tall = tall.transpose(1, 3, 0, 4, 2).reshape(planes, rows + PATCH, cols)
    broad = nets[2].reshape(broad_blocks, times, rows, slices, PATCH)
    broad = broad.transpose(1, 3, 2, 0, 4).reshape(planes, rows, cols + PATCH)
    return pad_lanes(both), pad_lanes(tall), pad_lanes(broad)


def join(offsets, weights, state, data_fit, both, tall, broad):
    agents, times, slices, rows, cols = state.shape
    vmem = pl.BlockSpec(memory_space=pltpu.VMEM)
    smem = pl.BlockSpec(memory_space=pltpu.SMEM)
    flat = state.reshape(agents, times * slices, rows, cols)
    out = pl.pallas_call(
        join_kernel,
        out_shape=jax.ShapeDtypeStruct(flat.shape, jnp.float32),
        in_specs=[smem, smem, vmem, vmem, vmem, vmem, vmem],
        out_specs=vmem,
        compiler_params=pltpu.CompilerParams(vmem_limit_bytes=32 * 2**20),
        name="join",
    )(offsets, weights, flat, data_fit.reshape(flat.shape[1:]), both, tall, broad)
    return out.reshape(state.shape)


def data_and_nets(
    volume, bin_index, bin_frac, measured, factor, patches, up_weight, down_weight
):
    angles = bin_index.shape[0]
    planes = volume.shape[0] * volume.shape[1]
    current = volume.reshape(planes, -1)
    tiles, agents, own = lax.axis_size("tile"), lax.axis_size("agent"), measured.shape[2]
    bins = tiles * agents * own // angles
    window = -(-(bin_index.shape[1] + bin_index.shape[2] + 2) // LANES) * LANES
    window = min(window, bins)
    lows = bin_index.reshape(angles, -1)
    fracs = bin_frac.reshape(angles, -1)
    corners = bin_index[:, :: bin_index.shape[1] - 1, :: bin_index.shape[2] - 1]
    starts = jnp.minimum(jnp.min(corners, axis=(1, 2)), bins - window)
    result, *nets = exchange(
        factor, window, starts, current, lows, fracs, measured.reshape(planes, own), patches,
        up_weight, down_weight, (bin_index.shape[1] // PATCH, bin_index.shape[2] // PATCH),
    )
    return result.reshape(volume.shape), nets


def shards(
    agent_state, measured, bin_index, bin_frac, patch_offsets, agent_weights, up_weight, down_weight
):
    row_count = agent_state.shape[3]
    col_count = agent_state.shape[4]
    tile_count = lax.axis_size("tile")
    agent_count = lax.axis_size("agent")
    full_rows = row_count * tile_count
    full_cols = col_count * agent_count
    angles = bin_index.shape[0]
    factor = 1.0 / math.sqrt(angles * (full_rows + full_cols))
    patches = make_patches(agent_state[1:].astype(jnp.bfloat16), patch_offsets)
    data_fit, nets = data_and_nets(
        agent_state[0], bin_index, bin_frac, measured, factor, patches, up_weight, down_weight
    )
    parts = spread_nets(nets, agent_state.shape[1:])
    state_next = join(patch_offsets, agent_weights, agent_state, data_fit, *parts)
    return (state_next, data_fit)


def solution(mesh):
    placed = (
        P(None, None, None, "tile", "agent"),
        P(None, None, ("tile", "agent")),
        P(None, "tile", "agent"),
        P(None, "tile", "agent"),
        P(),
        P(),
        P(None, None, "agent"),
        P(None, "agent", None),
    )
    return jax.shard_map(
        shards,
        mesh=mesh,
        in_specs=placed,
        out_specs=(P(None, None, None, "tile", "agent"), P(None, None, "tile", "agent")),
        check_vma=False,
    )
```
